128 devices in a mesh: lat: 8 (over z, x_hi), lon: 16 (over x_lo, y, core).
Axes of the slice: x: 4 (x_hi: 2, x_lo: 2; x = x_hi * 2 + x_lo), y: 4, z: 4, core: 2. Of those that a mesh axis runs over, the one named last changes fastest.
Arguments:
- adjoint_displacement: float32 [2, 8, 5, 640, 640], P(None, 'lat', None, 'lon'), may hold values from -0.08 to 0.08, as said below
- adjoint_velocity: float32 [2, 8, 5, 640, 640], P(None, 'lat', None, 'lon'), may hold values from -8 to 8, as said below
- bulk_modulus_field: bfloat16 [8, 5, 640, 640], P('lat', None, 'lon'), may hold values from 0.5 to 2
- density: bfloat16 [8, 5, 640, 640], P('lat', None, 'lon'), may hold values from 1 to 3
- forward_displacement: bfloat16 [2, 2, 8, 5, 640, 640], P(None, None, 'lat', None, 'lon'), may hold values from -8 to 8, as said below
- adjoint_traces: float32 [2, 3, 131072], P(None, None, ('lat', 'lon')), may hold values from -1.5 to 1.5
- receiver_owner: int32 [131072], P(('lat', 'lon')), may hold values from 0 to 127, as said below
- receiver_point: int32 [131072], P(('lat', 'lon')), may hold values from 0 to 127999
Outputs:
- final_velocity: float32 [2, 8, 5, 640, 640], P(None, 'lat', None, 'lon')
- modulus_kernel: float32 [8, 5, 640, 640], P('lat', None, 'lon')
The draws below stay inside these ranges and needn't reach their ends.
Inputs may be any that keep to these rules, and one draw needn't show every extreme that they name: `adjoint_displacement`: equal on all element points that lie on one grid point. `adjoint_velocity`: equal on all element points that lie on one grid point. `forward_displacement`: equal on all element points that lie on one grid point. `receiver_owner`: among the 1024 receivers of one device at most 32 name the same owner; one owner, drawn from the seed, is named by exactly 32 receivers of every device.
All inputs are finite; a program needn't handle non-finite values.
Results may differ from the reference program's by a relative error of at most 0.0003.
Values sent between devices are 32-bit elements; how exact they have to be, the bound alone decides.
No kernel may reach another device: no remote copies, remote signals or barrier semaphores. Data moves between devices by JAX's collectives and lax.ppermute only.
A program may use at most 320 MiB of HBM per device.

```python
import math
import jax
import jax.numpy as jnp
import numpy as np
from jax import lax

EX = 1
EY = 8
EZ = 128
RUNS = 2
RECEIVERS = 1024
STEPS = 2
LATITUDE_CELLS = 8
LONGITUDE_CELLS = 128
DEPTH_CELLS = 128
STATIONS = 131072
CAPACITY = 32
N_LON = 16
DEVICES = 128


def element_points(element_grid):
    x_index = (4 * jnp.arange(LATITUDE_CELLS)[:, None] + jnp.arange(5)[None, :]).reshape(-1)
    y_index = (4 * jnp.arange(LONGITUDE_CELLS)[:, None] + jnp.arange(5)[None, :]).reshape(-1)
    depth_position = (4 * jnp.arange(DEPTH_CELLS)[None, :] + jnp.arange(5)[:, None]).reshape(-1)
    selected_values = jnp.take(element_grid, x_index, axis=-3)
    selected_values = jnp.take(selected_values, y_index, axis=-2)
    selected_values = jnp.take(selected_values, depth_position, axis=-1)
    return selected_values.reshape(element_grid.shape[:-3] + (LATITUDE_CELLS, 5, 5 * LONGITUDE_CELLS, 5 * DEPTH_CELLS))


def node_field(key, leading_shape, scale):
    element_grid_shape = leading_shape + (4 * LATITUDE_CELLS + 1, 4 * LONGITUDE_CELLS + 1, 4 * DEPTH_CELLS + 1)
    gauss = jax.random.normal(jax.random.fold_in(key, 1), element_grid_shape, jnp.float32)
    element_grid = scale * jnp.clip(gauss, -8.0, 8.0)
    return element_points(element_grid)


def draw_adjoint_displacement(key, part):
    key = jax.random.fold_in(key, 11)
    return node_field(key, (RUNS,), 0.01)


def draw_adjoint_velocity(key, part):
    key = jax.random.fold_in(key, 12)
    return node_field(key, (RUNS,), 1.0)


def draw_forward_displacement(key, part):
    key = jax.random.fold_in(key, 13)
    return node_field(key, (STEPS, RUNS), 1.0).astype(jnp.bfloat16)


def draw_receiver_owner(key, part):
    key = jax.random.fold_in(key, 17)
    hot_owner = jax.random.randint(jax.random.fold_in(key, 1), (), 0, DEVICES).astype(jnp.int32)

    def one_block(block):
        block_key = jax.random.fold_in(key, block + 100)
        spread = jax.random.permutation(jax.random.fold_in(block_key, 1), (DEVICES - 1) * CAPACITY)[:RECEIVERS - CAPACITY]
        owners = (spread // CAPACITY).astype(jnp.int32)
        owners = owners + (owners >= hot_owner).astype(jnp.int32)
        joined = jnp.concatenate([jnp.full((CAPACITY,), hot_owner, jnp.int32), owners])
        order = jax.random.permutation(jax.random.fold_in(block_key, 2), RECEIVERS)
        return joined[order]
    return jax.vmap(one_block)(jnp.arange(DEVICES)).reshape(-1).astype(jnp.int32)


def with_ends(drawn, key, smallest, largest):
    place = [jax.random.randint(jax.random.fold_in(key, axis), (), 0, length) for axis, length in enumerate(drawn.shape)]
    widest = drawn.shape.index(max(drawn.shape))
    next_to = place[:widest] + [(place[widest] + 1) % drawn.shape[widest]] + place[widest + 1:]
    return drawn.at[tuple(place)].set(smallest).at[tuple(next_to)].set(largest)


def level_of(key, dims, split, low, high):
    def one(axis_at, blocks):
        draws = jax.random.uniform(jax.random.fold_in(jax.random.fold_in(key, 6), axis_at), (blocks,), jnp.float32, low / len(split), high / len(split))
        return jnp.repeat(jnp.exp(draws), dims[axis_at] // blocks).reshape((-1,) + (1,) * (len(dims) - axis_at - 1))

    loudness = one(*split[0])
    for cut in split[1:]:
        loudness = loudness * one(*cut)
    return loudness


def scatter_about(stream_key, dims, deviation, most, shards=(), held_as=jnp.bfloat16):
    result = jax.random.normal(stream_key, dims, jnp.float32) * deviation
    if len(shards) > 0:
        result = level_of(stream_key, dims, shards, -0.22, 0.18) * result
    return jnp.clip(result, min=-most, max=most).astype(held_as)


def setup_inputs(seed: int = 0) -> dict:
    arg_keys = jax.random.split(jax.random.key(seed), 9)
    adjoint_displacement = draw_adjoint_displacement(jax.random.fold_in(arg_keys[8], 71), 0)
    adjoint_velocity = draw_adjoint_velocity(jax.random.fold_in(arg_keys[8], 71), 0)
    bulk_modulus_field = jnp.clip(jnp.exp(math.log(2.0) - 1.3862944 * jax.random.uniform(arg_keys[2], (LATITUDE_CELLS, 5, 5 * LONGITUDE_CELLS, 5 * DEPTH_CELLS), jnp.float32) ** level_of(arg_keys[2], (LATITUDE_CELLS, 5, 5 * LONGITUDE_CELLS, 5 * DEPTH_CELLS), ((0, 8), (2, 16)), -0.2, 0.2)), 0.5, 2.0).astype(jnp.bfloat16)
    density = jnp.clip(jnp.exp(math.log(3.0) - 1.0986123 * jax.random.uniform(arg_keys[3], (LATITUDE_CELLS, 5, 5 * LONGITUDE_CELLS, 5 * DEPTH_CELLS), jnp.float32) ** level_of(arg_keys[3], (LATITUDE_CELLS, 5, 5 * LONGITUDE_CELLS, 5 * DEPTH_CELLS), ((0, 8), (2, 16)), -0.2, 0.2)), 1.0, 3.0).astype(jnp.bfloat16)
    forward_displacement = draw_forward_displacement(jax.random.fold_in(arg_keys[8], 71), 0)
    adjoint_traces = scatter_about(arg_keys[5], (RUNS, STEPS + 1, STATIONS), 0.1, 1.5, ((2, 128),), jnp.float32)
    receiver_owner = draw_receiver_owner(jax.random.fold_in(arg_keys[8], 71), 0)
    receiver_point = with_ends(jax.random.randint(arg_keys[7], (STATIONS,), 0, 125 * EX * EY * EZ), jax.random.fold_in(arg_keys[7], 1), 0, (125 * EX * EY * EZ) - 1).astype(jnp.int32)
    return {"adjoint_displacement": adjoint_displacement, "adjoint_velocity": adjoint_velocity, "bulk_modulus_field": bulk_modulus_field, "density": density, "forward_displacement": forward_displacement, "adjoint_traces": adjoint_traces, "receiver_owner": receiver_owner, "receiver_point": receiver_point}


time_step = 0.05
highest = lax.Precision.HIGHEST

def gll_tables():
    root_value = math.sqrt(3.0 / 7.0)
    gll_points = np.array([-1.0, -root_value, 0.0, root_value, 1.0])
    gll_weights = np.array([0.1, 49.0 / 90.0, 32.0 / 45.0, 49.0 / 90.0, 0.1])
    legendre = (35.0 * gll_points ** 4 - 30.0 * gll_points ** 2 + 3.0) / 8.0
    derivative = np.zeros((5, 5))
    for point_a in range(5):
        for point_b in range(5):
            if point_a != point_b:
                derivative[point_a, point_b] = legendre[point_a] / legendre[point_b] / (gll_points[point_a] - gll_points[point_b])
    derivative[0, 0] = -5.0
    derivative[4, 4] = 5.0
    weight_cube = gll_weights[:, None, None] * gll_weights[None, :, None] * gll_weights[None, None, :]
    return (jnp.asarray(derivative, jnp.float32), jnp.asarray(weight_cube.reshape(1, 1, 5, 1, 5, 5, 1), jnp.float32))

def element_view(field):
    count, blocks_x, unused, rows_y, depth_all = field.shape
    return field.reshape(count, blocks_x, 5, rows_y // 5, 5, 5, depth_all // 5)

def gradients(view, derivative):
    along_x = jnp.einsum('ai,rxiyjkz->rxayjkz', derivative, view, precision=highest)
    along_y = jnp.einsum('bj,rxiyjkz->rxiybkz', derivative, view, precision=highest)
    along_z = jnp.einsum('ck,rxiyjkz->rxiyjcz', derivative, view, precision=highest)
    return (along_x, along_y, along_z)

def stiffness(field, modulus, derivative, weight_cube):
    grads = gradients(element_view(field), derivative)
    scaled = weight_cube * element_view(modulus[None])
    force = jnp.einsum('ai,rxayjkz->rxiyjkz', derivative, scaled * grads[0], precision=highest)
    force = force + jnp.einsum('bj,rxiybkz->rxiyjkz', derivative, scaled * grads[1], precision=highest)
    force = force + jnp.einsum('ck,rxiyjcz->rxiyjkz', derivative, scaled * grads[2], precision=highest)
    return (force.reshape(field.shape), grads)

def kernel_term(grads, forward, modulus, derivative):
    forward_grads = gradients(element_view(forward.astype(jnp.float32)), derivative)
    total = grads[0] * forward_grads[0] + grads[1] * forward_grads[1] + grads[2] * forward_grads[2]
    summed = lax.optimization_barrier(jnp.sum(total, axis=0)) * element_view(modulus[None])[0]
    return summed.reshape(modulus.shape)

def local_mass(density, weight_cube):
    return (weight_cube * element_view(density.astype(jnp.float32)[None]))[0].reshape(density.shape)

def fold_faces(extended, axis_pos, blocks):
    length = extended.shape[axis_pos]
    outer_shape = extended.shape[:axis_pos]
    inner_shape = extended.shape[axis_pos + 1:]
    interior = lax.slice_in_dim(extended, 1, length - 1, axis=axis_pos)
    split_view = interior.reshape(outer_shape + (blocks, 5) + inner_shape)
    below_rim = lax.slice_in_dim(extended, 0, 1, axis=axis_pos)
    above_rim = lax.slice_in_dim(extended, length - 1, length, axis=axis_pos)
    low_face = lax.index_in_dim(split_view, 0, axis_pos + 1, keepdims=False)
    high_face = lax.index_in_dim(split_view, 4, axis_pos + 1, keepdims=False)
    from_below = jnp.concatenate([below_rim, lax.slice_in_dim(high_face, 0, blocks - 1, axis=axis_pos)], axis_pos)
    from_above = jnp.concatenate([lax.slice_in_dim(low_face, 1, blocks, axis=axis_pos), above_rim], axis_pos)
    middle = lax.slice_in_dim(split_view, 1, 4, axis=axis_pos + 1)
    joined = jnp.concatenate([jnp.expand_dims(low_face + from_below, axis_pos + 1), middle, jnp.expand_dims(high_face + from_above, axis_pos + 1)], axis_pos + 1)
    return joined.reshape(outer_shape + (blocks * 5,) + inner_shape)

def fold_depth(field):
    leading_shape = field.shape[:-1]
    depth = field.shape[-1] // 5
    split_view = field.reshape(leading_shape + (5, depth))
    low_face = split_view[..., 0, :]
    high_face = split_view[..., 4, :]
    zero_line = jnp.zeros(leading_shape + (1,), field.dtype)
    from_below = jnp.concatenate([zero_line, high_face[..., :-1]], -1)
    from_above = jnp.concatenate([low_face[..., 1:], zero_line], -1)
    joined = jnp.concatenate([(low_face + from_below)[..., None, :], split_view[..., 1:4, :], (high_face + from_above)[..., None, :]], -2)
    return joined.reshape(field.shape)

def assemble(field):
    count, blocks_x, unused, rows_y, depth_all = field.shape
    merged = field.reshape(count, blocks_x * 5, rows_y, depth_all)
    padded = jnp.pad(merged, ((0, 0), (1, 1), (1, 1), (0, 0)))
    merged = fold_faces(padded, 1, blocks_x)
    merged = fold_faces(merged, 2, rows_y // 5)
    return fold_depth(merged).reshape(field.shape)

def source_field(adjoint_traces, receiver_owner, receiver_point, time_index, field_shape):
    depth_all = 5 * EZ
    rows_y = 5 * EY
    index_depth = receiver_point % depth_all
    remain = receiver_point // depth_all
    index_row = remain % rows_y
    remain = remain // rows_y
    index_point = remain % 5
    index_block = remain // 5
    lat_index = receiver_owner // N_LON
    lon_index = receiver_owner % N_LON
    empty = jnp.zeros(field_shape, jnp.float32)
    return empty.at[:, (lat_index * EX + index_block).astype(jnp.int32), index_point.astype(jnp.int32), (lon_index * rows_y + index_row).astype(jnp.int32), index_depth.astype(jnp.int32)].add(adjoint_traces[:, time_index, :])

def reference(adjoint_displacement, adjoint_velocity, bulk_modulus_field, density, forward_displacement, adjoint_traces, receiver_owner, receiver_point):
    derivative, weight_cube = gll_tables()
    modulus = bulk_modulus_field.astype(jnp.float32)
    mass = assemble(local_mass(density, weight_cube)[None])[0]
    field_shape = adjoint_displacement.shape

    def forces_only(single):
        return stiffness(single[None], modulus, derivative, weight_cube)[0][0]

    def element_work(pair):
        force, grads = stiffness(pair[0][None], modulus, derivative, weight_cube)
        return (force[0], kernel_term(grads, pair[1][None], modulus, derivative))
    force = lax.map(forces_only, adjoint_displacement)
    acceleration = assemble(source_field(adjoint_traces, receiver_owner, receiver_point, 0, field_shape) - force) / mass
    displacement = adjoint_displacement
    velocity = adjoint_velocity
    kernel = jnp.zeros(modulus.shape, jnp.float32)
    for step_index in range(STEPS):
        displacement = displacement + time_step * velocity + 0.5 * time_step * time_step * acceleration
        velocity = velocity + 0.5 * time_step * acceleration
        force, terms = lax.map(element_work, (displacement, forward_displacement[step_index]))
        acceleration = assemble(source_field(adjoint_traces, receiver_owner, receiver_point, step_index + 1, field_shape) - force) / mass
        velocity = velocity + 0.5 * time_step * acceleration
        kernel = kernel - time_step * lax.optimization_barrier(jnp.sum(terms, axis=0))
    return (velocity, kernel)
```

```python
import functools
import math

import jax
import jax.numpy as jnp
import numpy as np
from jax import lax
from jax.experimental import pallas as pl
from jax.experimental.pallas import tpu as pltpu
from jax.sharding import PartitionSpec as P

time_step = 0.05
f32 = jnp.float32
bf16 = jnp.bfloat16
points = 125
padded = 128
slots = 32
face_tiles = 18
VMEM = pl.BlockSpec(memory_space=pltpu.VMEM)
SMEM = pl.BlockSpec(memory_space=pltpu.SMEM)


def gll_tables():
    root_value = math.sqrt(3.0 / 7.0)
    gll_points = np.array([-1.0, -root_value, 0.0, root_value, 1.0])
    gll_weights = np.array([0.1, 49.0 / 90.0, 32.0 / 45.0, 49.0 / 90.0, 0.1])
    legendre = (35.0 * gll_points**4 - 30.0 * gll_points**2 + 3.0) / 8.0
    derivative = np.zeros((5, 5))
    for a in range(5):
        for b in range(5):
            if a != b:
                derivative[a, b] = legendre[a] / legendre[b] / (gll_points[a] - gll_points[b])
    derivative[0, 0] = -5.0
    derivative[4, 4] = 5.0
    return derivative, gll_weights


derivative, gll_weights = gll_tables()
transposed = derivative.T


def weight(i, j, k):
    return float(gll_weights[i] * gll_weights[j] * gll_weights[k])


def apply5(matrix, u):
    odd = (u[0] - u[4], u[1] - u[3])
    even = (u[0] + u[4], u[1] + u[3])
    out = [None] * 5
    for a in (0, 1):
        p = float(0.5 * (matrix[a, 0] - matrix[a, 4])) * odd[0]
        p = p + float(0.5 * (matrix[a, 1] - matrix[a, 3])) * odd[1]
        m = float(0.5 * (matrix[a, 0] + matrix[a, 4])) * even[0]
        m = m + float(0.5 * (matrix[a, 1] + matrix[a, 3])) * even[1]
        m = m + float(matrix[a, 2]) * u[2]
        out[a] = p + m
        out[4 - a] = p - m
    out[2] = float(matrix[2, 0]) * odd[0] + float(matrix[2, 1]) * odd[1]
    return out


directions = ((5, 1, 25), (25, 1, 5), (25, 5, 1))


def for_lines(body):
    for direction, (outer, inner, step) in enumerate(directions):

        def block(t, carry, direction=direction, outer=outer, inner=inner, step=step):
            for line in range(5):
                base = t * outer + line * inner
                body(direction, [base + step * n for n in range(5)])
            return carry

        lax.fori_loop(0, 5, block, 0)


def sublane():
    return lax.broadcasted_iota(jnp.int32, (8, 128), 0)


def lane():
    return lax.broadcasted_iota(jnp.int32, (8, 128), 1)


def row_of(tile, index):
    return jnp.broadcast_to(tile[index : index + 1, :], (8, 128))


def column_of(tile, index):
    return jnp.broadcast_to(tile[:, index : index + 1], (8, 128))


def at(i, j, k):
    return (i * 5 + j) * 5 + k


def to_tiles(plane, put, wide):
    for i in range(5):
        rows = plane(i)
        for k in range(5):
            wide[i, k] = rows[:, k * 128 : (k + 1) * 128]
        for j in range(5):
            for k in range(5):
                put(at(i, j, k), wide[i, k, pl.ds(j, 8, stride=5), :])


def from_tiles(tile, put_plane, wide):
    for i in range(5):
        for j in range(5):
            for k in range(5):
                wide[i, k, pl.ds(j, 8, stride=5), :] = tile(i, j, k)
        for k in range(5):
            put_plane(i, k, wide[i, k])


def subtract_stiffness(d, f, e, wm):
    def line(direction, index):
        g = apply5(derivative, [d[e, n] for n in index])
        r = apply5(transposed, [g[a] * wm[index[a]] for a in range(5)])
        for a in range(5):
            f[e, index[a]] = f[e, index[a]] - r[a]

    for_lines(line)


def fold(get, put):
    sub, ln = sublane(), lane()
    for i in range(5):
        v = [[get(at(i, j, k)) for k in range(5)] for j in range(5)]
        for k in range(5):
            v[0][k] = v[0][k] + jnp.where(sub == 0, 0.0, pltpu.roll(v[4][k], 1, 0))
        for j in range(5):
            v[j][0] = v[j][0] + jnp.where(ln == 0, 0.0, pltpu.roll(v[j][4], 1, 1))
        for j in range(5):
            for k in range(5):
                if (j, k) == (0, 4) or j == 0 or k == 0:
                    put(at(i, j, k), v[j][k])


def emit_faces(get, c, face_low, face_high, row_low, row_high):
    sub, ln = sublane(), lane()
    for i, face in ((0, face_low), (4, face_high)):
        last_row = jnp.zeros((8, 128), f32)
        last_column = jnp.zeros((8, 128), f32)
        for k in range(5):
            last_row = jnp.where(sub == k, row_of(get(at(i, 4, k)), 7), last_row)
        for j in range(4):
            last_column = jnp.where(ln == j, column_of(get(at(i, j, 4)), 127), last_column)
            for k in range(4):
                face[c, j * 4 + k] = get(at(i, j, k))
        face[c, 16] = last_row
        face[c, 17] = last_column
    for i in range(5):
        low = jnp.zeros((8, 128), f32)
        high = jnp.zeros((8, 128), f32)
        for k in range(5):
            low = jnp.where(sub == k, row_of(get(at(i, 0, k)), 0), low)
            high = jnp.where(sub == k, row_of(get(at(i, 4, k)), 7), high)
        row_low[c, i] = low
        row_high[c, i] = high


def complete(get, i, c, flags, from_below, from_above, from_left, from_right):
    sub, ln = sublane(), lane()
    v = [[get(at(i, j, k)) for k in range(5)] for j in range(5)]
    if i in (0, 4):
        face = from_below if i == 0 else from_above
        keep = flags[0 if i == 0 else 1] > 0
        for j in range(4):
            for k in range(4):
                v[j][k] = v[j][k] + jnp.where(keep, face[c, j * 4 + k], 0.0)
        last_row, last_column = face[c, 16], face[c, 17]
        for k in range(5):
            v[4][k] = v[4][k] + jnp.where((sub == 7) & keep, row_of(last_row, k), 0.0)
        for j in range(4):
            v[j][4] = v[j][4] + jnp.where((ln == 127) & keep, column_of(last_column, j), 0.0)
    left, right = from_left[c, i], from_right[c, i]
    for k in range(5):
        v[0][k] = v[0][k] + jnp.where((sub == 0) & (flags[2] > 0), row_of(left, k), 0.0)
        v[4][k] = v[4][k] + jnp.where((sub == 7) & (flags[3] > 0), row_of(right, k), 0.0)
    for k in range(5):
        v[4][k] = jnp.where(sub == 7, v[4][k], pltpu.roll(v[0][k], 7, 0))
    for j in range(5):
        v[j][4] = jnp.where(ln == 127, v[j][4], pltpu.roll(v[j][0], 127, 1))
    return v


def pack_kernel(traces, owner, point, out):
    devices = out.shape[0] // 2
    receivers = owner.shape[1]
    p = point[...]
    hi = p >> 7
    lo = p & 127

    def divide(x, by):
        return jnp.floor((x.astype(f32) + 0.5) * (1.0 / by)).astype(jnp.int32)

    t = divide(hi, 5)
    k = hi - 5 * t
    i = divide(t, 40)
    row = t - 40 * i
    ey = divide(row, 5)
    j = row - 5 * ey
    place = ((((i * 5 + j) * 5 + k) * 8 + ey) * 128 + lo).astype(f32)
    rows = [traces[0, 0:1, :], traces[1, 0:1, :], place, traces[0, 1:2, :]]
    rows += [traces[1, 1:2, :], traces[0, 2:3, :], traces[1, 2:3, :], jnp.zeros((1, receivers), f32)]
    owned = lax.broadcasted_iota(jnp.int32, (devices, receivers), 0) == owner[...]
    owned = jnp.where(owned, 1.0, 0.0)
    before = lax.broadcasted_iota(jnp.int32, (128, 128), 0) < lax.broadcasted_iota(jnp.int32, (128, 128), 1)
    before = jnp.where(before, 1.0, 0.0).astype(bf16)
    carry = jnp.zeros((devices, 1), f32)
    ranks = []
    for chunk in range(receivers // 128):
        part = owned[:, chunk * 128 : (chunk + 1) * 128]
        earlier = jnp.dot(part.astype(bf16), before, preferred_element_type=f32) + carry
        ranks.append(jnp.sum(part * earlier, axis=0, keepdims=True))
        carry = carry + jnp.sum(part, axis=1, keepdims=True)
    rank = jnp.concatenate(ranks, axis=1).astype(jnp.int32)
    chosen = lax.broadcasted_iota(jnp.int32, (slots, receivers), 0) == rank
    owned = owned.astype(bf16)
    total = jnp.zeros((devices, 256), f32)
    left = rows
    for _ in range(3):
        pieces = [v.astype(bf16) for v in left]
        left = [v - q.astype(f32) for v, q in zip(left, pieces)]
        table = jnp.concatenate([jnp.where(chosen, q.astype(f32), 0.0) for q in pieces], axis=0)
        total = total + lax.dot_general(
            owned, table.astype(bf16), (((1,), (1,)), ((), ())), preferred_element_type=f32
        )
    out[pl.ds(0, devices, stride=2), :] = total[:, :128]
    out[pl.ds(1, devices, stride=2), :] = total[:, 128:]


def scatter(places, values, hi_rows, lo_rows, piece_rows, left_side, right_side, store):
    place = places.astype(jnp.int32)
    hi_rows[...] = place >> 7
    lo_rows[...] = place & 127
    count = len(values)
    for c, v in enumerate(values):
        upper = v.astype(bf16).astype(f32)
        piece_rows[2 * c] = upper
        piece_rows[2 * c + 1] = v - upper
    index = lax.broadcasted_iota(jnp.int32, (128, 128), 0)

    def fill(r, carry):
        where = pl.ds(pl.multiple_of(r * 128, 128), 128)
        hi = hi_rows[pl.ds(r, 1), :]
        lo = lo_rows[pl.ds(r, 1), :]
        for m in range(8):
            left_side[m * 128 : (m + 1) * 128, where] = jnp.where(index + m * 128 == hi, 1.0, 0.0).astype(bf16)
        same = index == lo
        for n in range(2 * count):
            right_side[n * 128 : (n + 1) * 128, where] = jnp.where(same, piece_rows[n, pl.ds(r, 1), :], 0.0).astype(bf16)
        return carry

    lax.fori_loop(0, slots, fill, 0)

    def tile(m, carry):
        rows = pl.ds(pl.multiple_of(m * 256, 256), 256)
        for c in range(count):
            both = lax.dot_general(
                left_side[rows, :],
                right_side[c * 256 : (c + 1) * 256, :],
                (((1,), (1,)), ((), ())),
                preferred_element_type=f32,
            )
            store(m, c, both[:, :128] + both[:, 128:])
        return carry

    lax.fori_loop(0, 4, tile, 0)


def start_kernel(d0, v0, modulus, density, d_out, v_out, wm, mass, kd, wide):
    def put_event(e, carry):
        for source, target in ((d0, d_out), (v0, v_out)):

            def put_field(n, value, target=target):
                target[e, n] = value

            to_tiles(lambda i, source=source: source[e, i], put_field, wide)
        return carry

    lax.fori_loop(0, 2, put_event, 0)
    for source, target in ((modulus, wm), (density, mass)):

        def put_weighted(n, value, target=target):
            target[n] = value * weight(n // 25, n // 5 % 5, n % 5)

        to_tiles(lambda i, source=source: source[i].astype(f32), put_weighted, wide)

    def put(n, value):
        mass[n] = value

    fold(lambda n: mass[n], put)

    def clear(n, carry):
        kd[0, n] = jnp.zeros((8, 128), f32)
        kd[1, n] = jnp.zeros((8, 128), f32)
        return carry

    lax.fori_loop(0, points, clear, 0)

    def event(e, carry):
        subtract_stiffness(d_out, kd, e, wm)
        return carry

    lax.fori_loop(0, 2, event, 0)


def first_force_kernel(got, kd, mass, f, face_low, face_high, row_low, row_high, sums, hi_rows, lo_rows, piece_rows, left_side, right_side):
    devices = got.shape[0] // 2
    first = got[pl.ds(0, devices, stride=2), :].T

    def store(m, c, value):
        sums[c, pl.ds(m * 32, 32)] = value.reshape(32, 8, 128)

    scatter(first[64:96], [first[0:32], first[32:64]], hi_rows, lo_rows, piece_rows, left_side, right_side, store)

    def event(e, carry):
        def get(n):
            return kd[e, n] + sums[e, n]

        def copy(n, c):
            f[e, n] = get(n)
            return c

        lax.fori_loop(0, points, copy, 0)

        def put(n, value):
            f[e, n] = value

        fold(lambda n: f[e, n], put)
        emit_faces(lambda n: f[e, n], e, face_low, face_high, row_low, row_high)
        return carry

    lax.fori_loop(0, 2, event, 0)
    emit_faces(lambda n: mass[n], 2, face_low, face_high, row_low, row_high)


def later_sources_kernel(got, s1, s2, hi_rows, lo_rows, piece_rows, left_side, right_side):
    devices = got.shape[0] // 2
    first = got[pl.ds(0, devices, stride=2), :].T
    second = got[pl.ds(1, devices, stride=2), :].T

    def store(m, c, value):
        target = s1 if c < 2 else s2
        target[c % 2, pl.ds(m * 32, 32)] = value.reshape(32, 8, 128)

    values = [first[96:128], second[0:32], second[32:64], second[64:96]]
    scatter(first[64:96], values, hi_rows, lo_rows, piece_rows, left_side, right_side, store)


def rows_kernel(flags, from_below, from_above, row_low, row_high, low_out, high_out):
    sub, ln = sublane(), lane()
    for c in range(row_low.shape[0]):
        for i in range(5):
            low, high = row_low[c, i], row_high[c, i]
            if i in (0, 4):
                face = from_below if i == 0 else from_above
                keep = flags[0 if i == 0 else 1] > 0
                extra = jnp.zeros((8, 128), f32)
                for k in range(4):
                    extra = jnp.where(sub == k, row_of(face[c, k], 0), extra)
                corner = jnp.broadcast_to(face[c, 17][0:1, 0:1], (8, 128))
                extra = jnp.where((sub == 4) & (ln == 127), corner, extra)
                low = low + jnp.where(keep, extra, 0.0)
                high = high + jnp.where(keep, face[c, 16], 0.0)
            low_out[c, i] = low
            high_out[c, i] = high


def step_kernel(first, *refs):
    if first:
        flags, f, below, above, left, right, d, q, source, wm, mass = refs[:11]
        d_out, q_out, inverse, f_out, face_low, face_high, row_low, row_high = refs[11:]
        for i in range(5):
            v = complete(lambda n: mass[n], i, 2, flags, below, above, left, right)
            for j in range(5):
                for k in range(5):
                    inverse[at(i, j, k)] = 1.0 / v[j][k]
    else:
        flags, f, below, above, left, right, d, q, source, wm, inverse = refs[:11]
        d_out, q_out, f_out, face_low, face_high, row_low, row_high = refs[11:]
    share = 0.5 * time_step if first else time_step

    def event(e, carry):
        for i in range(5):
            v = complete(lambda n: f[e, n], i, e, flags, below, above, left, right)
            for j in range(5):
                for k in range(5):
                    n = at(i, j, k)
                    q_new = q[e, n] + share * (v[j][k] * inverse[n])
                    q_out[e, n] = q_new
                    d_out[e, n] = d[e, n] + time_step * q_new

        def copy(n, c):
            f_out[e, n] = source[e, n]
            return c

        lax.fori_loop(0, points, copy, 0)
        subtract_stiffness(d_out, f_out, e, wm)

        def put(n, value):
            f_out[e, n] = value

        fold(lambda n: f_out[e, n], put)
        emit_faces(lambda n: f_out[e, n], e, face_low, face_high, row_low, row_high)
        return carry

    lax.fori_loop(0, 2, event, 0)


def last_kernel(flags, f, below, above, left, right, q, inverse, velocity, wide):
    def event(e, carry):
        for i in range(5):
            v = complete(lambda n: f[e, n], i, e, flags, below, above, left, right)
            for j in range(5):
                for k in range(5):
                    n = at(i, j, k)
                    wide[i, k, pl.ds(j, 8, stride=5), :] = q[e, n] + 0.5 * time_step * (v[j][k] * inverse[n])
            for k in range(5):
                velocity[e, i, :, k * 128 : (k + 1) * 128] = wide[i, k]
        return carry

    lax.fori_loop(0, 2, event, 0)


def correlate(d, forward, total, wide, tiles):
    def event(e, carry):
        def put(n, value):
            tiles[n] = value

        to_tiles(lambda i: forward[e, i].astype(f32), put, wide)

        def line(direction, index):
            g = apply5(derivative, [d[e, n] for n in index])
            h = apply5(derivative, [tiles[n] for n in index])
            for a in range(5):
                total[index[a]] = total[index[a]] + g[a] * h[a]

        for_lines(line)
        return carry

    lax.fori_loop(0, 2, event, 0)


def first_kernel_term(d, forward, total, wide, tiles):
    def clear(n, carry):
        total[n] = jnp.zeros((8, 128), f32)
        return carry

    lax.fori_loop(0, points, clear, 0)
    correlate(d, forward, total, wide, tiles)


def last_kernel_term(d, forward, before, wm, out, total, wide, tiles):
    def copy(n, carry):
        total[n] = before[n]
        return carry

    lax.fori_loop(0, points, copy, 0)
    correlate(d, forward, total, wide, tiles)

    def tile(i, j, k):
        return total[at(i, j, k)] * wm[at(i, j, k)] * (-time_step / weight(i, j, k))

    def put_plane(i, k, rows):
        out[i, :, k * 128 : (k + 1) * 128] = rows

    from_tiles(tile, put_plane, wide)


def call(kernel, name, out_shapes, args, scratch=(), specs=None, flops=10**6, moved=4 * 10**6):
    return pl.pallas_call(
        kernel,
        name=name,
        out_shape=[jax.ShapeDtypeStruct(s, f32) for s in out_shapes],
        in_specs=specs or [VMEM] * len(args),
        out_specs=[VMEM] * len(out_shapes),
        scratch_shapes=list(scratch),
        compiler_params=pltpu.CompilerParams(vmem_limit_bytes=56 * 2**20),
        cost_estimate=pl.CostEstimate(flops=flops, bytes_accessed=moved, transcendentals=0),
    )(*args)


def swap(low, high, axis):
    count = lax.axis_size(axis)
    up = [(n, (n + 1) % count) for n in range(count)]
    down = [(b, a) for a, b in up]
    return lax.ppermute(high, axis, up), lax.ppermute(low, axis, down)


def on_device(d0, v0, modulus, density, forward, traces, owner, point):
    lat, lon = lax.axis_index("lat"), lax.axis_index("lon")
    lat_count, lon_count = lax.axis_size("lat"), lax.axis_size("lon")
    devices = lat_count * lon_count
    flags = jnp.stack([lat > 0, lat < lat_count - 1, lon > 0, lon < lon_count - 1]).astype(jnp.int32)
    field = (2, points, 8, 128)
    one = (points, 8, 128)
    wide_field = (2, padded, 8, 128)
    native = d0.shape
    d0, v0 = d0.reshape(2, 5, 40, 640), v0.reshape(2, 5, 40, 640)
    kernel_shape = modulus.shape
    modulus, density = modulus.reshape(5, 40, 640), density.reshape(5, 40, 640)
    forward = forward.reshape(2, 2, 5, 40, 640)
    receivers = owner.shape[0]

    def faces(channels):
        return [(channels, face_tiles, 8, 128)] * 2 + [(channels, 5, 8, 128)] * 2

    (packed,) = call(
        pack_kernel, "pack", [(2 * devices, 128)], (traces, owner.reshape(1, receivers), point.reshape(1, receivers))
    )
    got = lax.all_to_all(packed.reshape(devices, 2, 128), ("lat", "lon"), 0, 0, tiled=True)
    got = got.reshape(2 * devices, 128)
    wide = pltpu.VMEM((5, 5, 40, 128), f32)
    tiles = pltpu.VMEM(one, f32)
    d, q, wm, mass, kd = call(
        start_kernel, "start", [field, field, one, one, field], (d0, v0, modulus, density), [wide], flops=10**8
    )

    def scatter_scratch(count):
        return [
            pltpu.VMEM((slots, devices), jnp.int32),
            pltpu.VMEM((slots, devices), jnp.int32),
            pltpu.VMEM((2 * count, slots, devices), f32),
            pltpu.VMEM((1024, slots * devices), bf16),
            pltpu.VMEM((256 * count, slots * devices), bf16),
        ]

    f, *edges = call(
        first_force_kernel,
        "first_force",
        [field] + faces(3),
        (got, kd, mass),
        [pltpu.VMEM(wide_field, f32)] + scatter_scratch(2),
        flops=4 * 10**9,
    )
    s1, s2 = call(
        later_sources_kernel, "later_sources", [wide_field, wide_field], (got,), scatter_scratch(4), flops=8 * 10**9
    )

    def exchange(edges):
        face_low, face_high, row_low, row_high = edges
        below, above = swap(face_low, face_high, "lat")
        low, high = call(
            rows_kernel,
            "rows",
            [row_low.shape] * 2,
            (flags, below, above, row_low, row_high),
            specs=[SMEM] + [VMEM] * 4,
            moved=4 * 10**5,
        )
        left, right = swap(low, high, "lon")
        return below, above, left, right

    specs = [SMEM] + [VMEM] * 10
    received = exchange(edges)
    d, q, inverse, f, *edges = call(
        functools.partial(step_kernel, True),
        "first_step",
        [field, field, one, field] + faces(2),
        (flags, f, *received, d, q, s1, wm, mass),
        specs=specs,
        flops=10**8,
    )
    (term,) = call(first_kernel_term, "first_term", [one], (d, forward[0]), [wide, tiles], flops=10**8)
    received = exchange(edges)
    d, q, f, *edges = call(
        functools.partial(step_kernel, False),
        "second_step",
        [field, field, field] + faces(2),
        (flags, f, *received, d, q, s2, wm, inverse),
        specs=specs,
        flops=10**8,
    )
    (kernel,) = call(
        last_kernel_term, "last_term", [(5, 40, 640)], (d, forward[1], term, wm), [tiles, wide, tiles], flops=10**8
    )
    received = exchange(edges)
    (velocity,) = call(
        last_kernel, "last", [(2, 5, 40, 640)], (flags, f, *received, q, inverse), [wide], [SMEM] + [VMEM] * 7
    )
    return velocity.reshape(native), kernel.reshape(kernel_shape)


def solution(mesh):
    placed = (
        P(None, "lat", None, "lon", None),
        P(None, "lat", None, "lon", None),
        P("lat", None, "lon", None),
        P("lat", None, "lon", None),
        P(None, None, "lat", None, "lon", None),
        P(None, None, ("lat", "lon")),
        P(("lat", "lon")),
        P(("lat", "lon")),
    )
    return jax.shard_map(
        on_device,
        mesh=mesh,
        in_specs=placed,
        out_specs=(P(None, "lat", None, "lon", None), P("lat", None, "lon", None)),
        check_vma=False,
    )
```

```python
import functools
import math

import jax
import jax.numpy as jnp
import numpy as np
from jax import lax
from jax.experimental import pallas as pl
from jax.experimental.pallas import tpu as pltpu
from jax.sharding import PartitionSpec as P

time_step = 0.05
f32 = jnp.float32
bf16 = jnp.bfloat16
points = 125
padded = 128
slots = 32
face_tiles = 18
kept_tiles = 12288
VMEM = pl.BlockSpec(memory_space=pltpu.VMEM)
SMEM = pl.BlockSpec(memory_space=pltpu.SMEM)
HBM = pl.BlockSpec(memory_space=pltpu.HBM)
ANY = pl.BlockSpec(memory_space=pl.ANY)


def gll_tables():
    root_value = math.sqrt(3.0 / 7.0)
    gll_points = np.array([-1.0, -root_value, 0.0, root_value, 1.0])
    gll_weights = np.array([0.1, 49.0 / 90.0, 32.0 / 45.0, 49.0 / 90.0, 0.1])
    legendre = (35.0 * gll_points**4 - 30.0 * gll_points**2 + 3.0) / 8.0
    derivative = np.zeros((5, 5))
    for a in range(5):
        for b in range(5):
            if a != b:
                derivative[a, b] = legendre[a] / legendre[b] / (gll_points[a] - gll_points[b])
    derivative[0, 0] = -5.0
    derivative[4, 4] = 5.0
    return derivative, gll_weights


derivative, gll_weights = gll_tables()
transposed = derivative.T


def weight(i, j, k):
    return float(gll_weights[i] * gll_weights[j] * gll_weights[k])


def apply5(matrix, u):
    odd = (u[0] - u[4], u[1] - u[3])
    even = (u[0] + u[4], u[1] + u[3])
    out = [None] * 5
    for a in (0, 1):
        p = float(0.5 * (matrix[a, 0] - matrix[a, 4])) * odd[0]
        p = p + float(0.5 * (matrix[a, 1] - matrix[a, 3])) * odd[1]
        m = float(0.5 * (matrix[a, 0] + matrix[a, 4])) * even[0]
        m = m + float(0.5 * (matrix[a, 1] + matrix[a, 3])) * even[1]
        m = m + float(matrix[a, 2]) * u[2]
        out[a] = p + m
        out[4 - a] = p - m
    out[2] = float(matrix[2, 0]) * odd[0] + float(matrix[2, 1]) * odd[1]
    return out


directions = ((5, 1, 25), (25, 1, 5), (25, 5, 1))


def for_lines(body, directions):
    for outer, inner, step in directions:
        for t in range(5):
            for line in range(5):
                base = t * outer + line * inner
                body([base + step * n for n in range(5)])


def sublane():
    return lax.broadcasted_iota(jnp.int32, (8, 128), 0)


def lane():
    return lax.broadcasted_iota(jnp.int32, (8, 128), 1)


def row_of(tile, index):
    return jnp.broadcast_to(tile[index : index + 1, :], (8, 128))


def column_of(tile, index):
    return jnp.broadcast_to(tile[:, index : index + 1], (8, 128))


def at(i, j, k):
    return (i * 5 + j) * 5 + k


def to_tiles(plane, put, wide):
    for i in range(5):
        rows = plane(i)
        for k in range(5):
            wide[i, k] = rows[:, k * 128 : (k + 1) * 128]
        for j in range(5):
            for k in range(5):
                put(at(i, j, k), wide[i, k, pl.ds(j, 8, stride=5), :])


def from_tiles(tile, put_plane, wide):
    for i in range(5):
        for j in range(5):
            for k in range(5):
                wide[i, k, pl.ds(j, 8, stride=5), :] = tile(i, j, k)
        for k in range(5):
            put_plane(i, k, wide[i, k])


def force(d, f, e, wm, source):
    def line(index, before):
        g = apply5(derivative, [d[e, n] for n in index])
        r = apply5(transposed, [g[a] * wm[index[a]] for a in range(5)])
        for a in range(5):
            f[e, index[a]] = before(index[a]) - r[a]

    for_lines(lambda index: line(index, source), directions[:1])
    for_lines(lambda index: line(index, lambda n: f[e, n]), directions[1:])


def fold(get, put, every=False):
    sub, ln = sublane(), lane()
    for i in range(5):
        v = [[get(at(i, j, k)) for k in range(5)] for j in range(5)]
        for k in range(5):
            v[0][k] = v[0][k] + jnp.where(sub == 0, 0.0, pltpu.roll(v[4][k], 1, 0))
        for j in range(5):
            v[j][0] = v[j][0] + jnp.where(ln == 0, 0.0, pltpu.roll(v[j][4], 1, 1))
        for j in range(5):
            for k in range(5):
                if every or j == 0 or k == 0:
                    put(at(i, j, k), v[j][k])


def emit_faces(get, c, face_low, face_high, row_low, row_high):
    lead = () if c is None else (c,)
    sub, ln = sublane(), lane()
    for i, face in ((0, face_low), (4, face_high)):
        last_row = jnp.zeros((8, 128), f32)
        last_column = jnp.zeros((8, 128), f32)
        for k in range(5):
            last_row = jnp.where(sub == k, row_of(get(at(i, 4, k)), 7), last_row)
        for j in range(4):
            last_column = jnp.where(ln == j, column_of(get(at(i, j, 4)), 127), last_column)
            for k in range(4):
                face[lead + (j * 4 + k,)] = get(at(i, j, k))
        face[lead + (16,)] = last_row
        face[lead + (17,)] = last_column
    for i in range(5):
        low = jnp.zeros((8, 128), f32)
        high = jnp.zeros((8, 128), f32)
        for k in range(5):
            low = jnp.where(sub == k, row_of(get(at(i, 0, k)), 0), low)
            high = jnp.where(sub == k, row_of(get(at(i, 4, k)), 7), high)
        row_low[lead + (i,)] = low
        row_high[lead + (i,)] = high


def complete(get, i, c, flags, from_below, from_above, from_even, from_odd):
    sub, ln = sublane(), lane()
    v = [[get(at(i, j, k)) for k in range(5)] for j in range(5)]
    if i in (0, 4):
        face = from_below if i == 0 else from_above
        keep = flags[0 if i == 0 else 1] > 0
        for j in range(4):
            for k in range(4):
                v[j][k] = v[j][k] + jnp.where(keep, face[c, j * 4 + k], 0.0)
        last_row, last_column = face[c, 16], face[c, 17]
        for k in range(5):
            v[4][k] = v[4][k] + jnp.where((sub == 7) & keep, row_of(last_row, k), 0.0)
        for j in range(4):
            v[j][4] = v[j][4] + jnp.where((ln == 127) & keep, column_of(last_column, j), 0.0)
    left = jnp.where(flags[4] > 0, from_odd[c, i], from_even[c, i])
    right = jnp.where(flags[4] > 0, from_even[c, i], from_odd[c, i])
    for k in range(5):
        v[0][k] = v[0][k] + jnp.where((sub == 0) & (flags[2] > 0), row_of(left, k), 0.0)
        v[4][k] = v[4][k] + jnp.where((sub == 7) & (flags[3] > 0), row_of(right, k), 0.0)
    for k in range(5):
        v[4][k] = jnp.where(sub == 7, v[4][k], pltpu.roll(v[0][k], 7, 0))
    for j in range(5):
        v[j][4] = jnp.where(ln == 127, v[j][4], pltpu.roll(v[j][0], 127, 1))
    return v


def pack_kernel(traces_in, owner_in, point_in, out, traces, owner, point, sems):
    pairs = ((traces_in, traces), (owner_in, owner), (point_in, point))
    copies = [pltpu.make_async_copy(a, b, sems.at[n]) for n, (a, b) in enumerate(pairs)]
    for copy in copies:
        copy.start()
    for copy in copies:
        copy.wait()
    devices = out.shape[0] // 2
    receivers = owner.shape[1]
    p = point[...]
    hi = p >> 7
    lo = p & 127

    def divide(x, by):
        return jnp.floor((x.astype(f32) + 0.5) * (1.0 / by)).astype(jnp.int32)

    t = divide(hi, 5)
    k = hi - 5 * t
    i = divide(t, 40)
    row = t - 40 * i
    ey = divide(row, 5)
    j = row - 5 * ey
    place = ((((i * 5 + j) * 5 + k) * 8 + ey) * 128 + lo).astype(f32)
    rows = [traces[0, 0:1, :], traces[0, 1:2, :], place, traces[1, 0:1, :]]
    rows += [traces[1, 1:2, :], traces[2, 0:1, :], traces[2, 1:2, :], jnp.zeros((1, receivers), f32)]
    owned = lax.broadcasted_iota(jnp.int32, (devices, receivers), 0) == owner[...]
    owned = jnp.where(owned, 1.0, 0.0)
    before = lax.broadcasted_iota(jnp.int32, (128, 128), 0) < lax.broadcasted_iota(jnp.int32, (128, 128), 1)
    before = jnp.where(before, 1.0, 0.0).astype(bf16)
    carry = jnp.zeros((devices, 1), f32)
    ranks = []
    for chunk in range(receivers // 128):
        part = owned[:, chunk * 128 : (chunk + 1) * 128]
        earlier = jnp.dot(part.astype(bf16), before, preferred_element_type=f32) + carry
        ranks.append(jnp.sum(part * earlier, axis=0, keepdims=True))
        carry = carry + jnp.sum(part, axis=1, keepdims=True)
    rank = jnp.concatenate(ranks, axis=1).astype(jnp.int32)
    chosen = lax.broadcasted_iota(jnp.int32, (slots, receivers), 0) == rank
    owned = owned.astype(bf16)
    total = jnp.zeros((devices, 256), f32)
    left = rows
    for _ in range(3):
        pieces = [v.astype(bf16) for v in left]
        left = [v - q.astype(f32) for v, q in zip(left, pieces)]
        table = jnp.concatenate([jnp.where(chosen, q.astype(f32), 0.0) for q in pieces], axis=0)
        total = total + lax.dot_general(
            owned, table.astype(bf16), (((1,), (1,)), ((), ())), preferred_element_type=f32
        )
    out[pl.ds(0, devices, stride=2), :] = total[:, :128]
    out[pl.ds(1, devices, stride=2), :] = total[:, 128:]


def scatter(places, values, hi_rows, lo_rows, piece_rows, left_side, right_side, store):
    place = places.astype(jnp.int32)
    hi_rows[...] = (place >> 7).astype(f32)
    lo_rows[...] = (place & 127).astype(f32)
    count = len(values)
    for c, v in enumerate(values):
        upper = v.astype(bf16).astype(f32)
        piece_rows[2 * c] = upper
        piece_rows[2 * c + 1] = v - upper
    index = [lax.broadcasted_iota(jnp.int32, (16, 128), 0).astype(f32) + 16.0 * g for g in range(8)]
    index = [x.astype(bf16) for x in index]
    one, zero = jnp.ones((16, 128), bf16), jnp.zeros((16, 128), bf16)

    def fill_right(r):
        where = slice(r * 128, r * 128 + 128)
        lo = jnp.broadcast_to(lo_rows[r : r + 1, :], (16, 128)).astype(bf16)
        pieces = [jnp.broadcast_to(piece_rows[n, r : r + 1, :], (16, 128)).astype(bf16) for n in range(2 * count)]
        for g in range(8):
            same = index[g] == lo
            for n in range(2 * count):
                at_row = n * 128 + g * 16
                right_side[at_row : at_row + 16, where] = jnp.where(same, pieces[n], zero)

    def fill_left(r, m):
        where = slice(r * 128, r * 128 + 128)
        hi = jnp.broadcast_to(hi_rows[r : r + 1, :], (16, 128))
        part = (hi - 128.0 * m).astype(bf16)
        for g in range(8):
            left_side[m * 128 + g * 16 : m * 128 + g * 16 + 16, where] = jnp.where(index[g] == part, one, zero)

    def fill_tile(m):
        for r in range(slots):
            fill_left(r, 2 * m)
            fill_left(r, 2 * m + 1)

    for r in range(slots):
        fill_right(r)
    fill_tile(0)
    for m in range(4):
        if m < 3:
            fill_tile(m + 1)
        for c in range(count):
            both = lax.dot_general(
                left_side[m * 256 : m * 256 + 256, :],
                right_side[c * 256 : c * 256 + 256, :],
                (((1,), (1,)), ((), ())),
                preferred_element_type=f32,
            )
            store(c, m, both[:, :128] + both[:, 128:])


def start_kernel(d_in, v_in, k_in, m_in, d_out, v_out, wm_out, mass_out, kept, *scratch):
    d0, v0, modulus, density, d, v, wm, mass, kd, edges, wide, sems = scratch
    copies = []

    def copy(source, target):
        copies.append(pltpu.make_async_copy(source, target, sems.at[len(copies)]))
        copies[-1].start()
        return copies[-1]

    loads = [copy(k_in, modulus), copy(d_in.at[0], d0.at[0]), copy(d_in.at[1], d0.at[1])]
    loads += [copy(m_in, density), copy(v_in, v0)]

    def weighted(target):
        def put(n, value):
            target[n] = value * weight(n // 25, n // 5 % 5, n % 5)

        return put

    loads[0].wait()
    to_tiles(lambda i: modulus[i].astype(f32), weighted(wm), wide)
    copy(wm, wm_out)
    for e in range(2):

        def put_d(n, value, e=e):
            d[e, n] = value

        loads[1 + e].wait()
        to_tiles(lambda i, e=e: d0[e, i], put_d, wide)
        copy(d.at[e], d_out.at[e])
        force(d, kd, e, wm, lambda n: 0.0)
        copy(kd.at[e], kept.at[e * points : e * points + points])
    loads[3].wait()
    to_tiles(lambda i: density[i].astype(f32), weighted(mass), wide)

    def put_mass(n, value):
        mass[n] = value

    fold(lambda n: mass[n], put_mass)
    copy(mass, mass_out)
    low, high, row_low, row_high = edges.at[0:18], edges.at[18:36], edges.at[36:41], edges.at[41:46]
    emit_faces(lambda n: mass[n], None, low, high, row_low, row_high)
    copy(edges, kept.at[2 * points : 2 * points + 46])
    loads[4].wait()
    for e in range(2):

        def put_v(n, value, e=e):
            v[e, n] = value

        to_tiles(lambda i, e=e: v0[e, i], put_v, wide)
        copy(v.at[e], v_out.at[e])
    for pending in copies[len(loads) :]:
        pending.wait()


def first_force_kernel(got, kept, f, face_low, face_high, row_low, row_high, kd, sems, *scratch):
    edges = kept.at[2 * points : 2 * points + 46]
    pairs = ((kept.at[0:points], kd.at[0]), (kept.at[points : 2 * points], kd.at[1]))
    pairs += ((edges.at[0:18], face_low.at[2]), (edges.at[18:36], face_high.at[2]))
    pairs += ((edges.at[36:41], row_low.at[2]), (edges.at[41:46], row_high.at[2]))
    copies = [pltpu.make_async_copy(a, b, sems.at[n]) for n, (a, b) in enumerate(pairs)]
    for copy in copies:
        copy.start()
    devices = got.shape[0] // 2
    first = got[pl.ds(0, devices, stride=2), :].T

    def store(c, m, value):
        count = min(32, points - 32 * m)
        f[c, 32 * m : 32 * m + count] = value.reshape(32, 8, 128)[:count]

    scatter(first[64:96], [first[0:32], first[32:64]], *scratch, store)
    for copy in copies:
        copy.wait()

    def event(e, carry):
        def put(n, value):
            f[e, n] = value

        fold(lambda n: f[e, n] + kd[e, n], put, every=True)
        emit_faces(lambda n: f[e, n], e, face_low, face_high, row_low, row_high)
        return carry

    lax.fori_loop(0, 2, event, 0)


def source_kernel(step, got, order, s, token, *scratch):
    devices = got.shape[0] // 2
    first = got[pl.ds(0, devices, stride=2), :].T
    second = got[pl.ds(1, devices, stride=2), :].T
    token[...] = jnp.zeros_like(token)

    def store(c, m, value):
        s[c, 32 * m : 32 * m + 32] = value.reshape(32, 8, 128)

    values = [first[96:128], second[0:32]] if step == 1 else [second[32:64], second[64:96]]
    scatter(first[64:96], values, *scratch, store)


def rows_kernel(flags, from_below, from_above, row_low, row_high, order, even_out, odd_out):
    sub, ln = sublane(), lane()
    for c in range(row_low.shape[0]):
        for i in range(5):
            low, high = row_low[c, i], row_high[c, i]
            if i in (0, 4):
                face = from_below if i == 0 else from_above
                keep = flags[0 if i == 0 else 1] > 0
                extra = jnp.zeros((8, 128), f32)
                for k in range(4):
                    extra = jnp.where(sub == k, row_of(face[c, k], 0), extra)
                corner = jnp.broadcast_to(face[c, 17][0:1, 0:1], (8, 128))
                extra = jnp.where((sub == 4) & (ln == 127), corner, extra)
                low = low + jnp.where(keep, extra, 0.0)
                high = high + jnp.where(keep, face[c, 16], 0.0)
            even_out[c, i] = jnp.where(flags[4] > 0, high, low)
            odd_out[c, i] = jnp.where(flags[4] > 0, low, high)


def step_kernel(first, *refs):
    if first:
        flags, f, below, above, left, right, d, q, source, wm, mass = refs[:11]
        d_out, q_out, inverse, f_out, face_low, face_high, row_low, row_high = refs[11:]
        for i in range(5):
            v = complete(lambda n: mass[n], i, 2, flags, below, above, left, right)
            for j in range(5):
                for k in range(5):
                    inverse[at(i, j, k)] = 1.0 / v[j][k]
    else:
        flags, f, below, above, left, right, d, q, source, wm, inverse = refs[:11]
        d_out, q_out, f_out, face_low, face_high, row_low, row_high = refs[11:]
    share = 0.5 * time_step if first else time_step

    def event(e, carry):
        for i in range(5):
            v = complete(lambda n: f[e, n], i, e, flags, below, above, left, right)
            for j in range(5):
                for k in range(5):
                    n = at(i, j, k)
                    q_new = q[e, n] + share * (v[j][k] * inverse[n])
                    q_out[e, n] = q_new
                    d_out[e, n] = d[e, n] + time_step * q_new

        force(d_out, f_out, e, wm, lambda n: source[e, n])

        def put(n, value):
            f_out[e, n] = value

        fold(lambda n: f_out[e, n], put)
        emit_faces(lambda n: f_out[e, n], e, face_low, face_high, row_low, row_high)
        return carry

    lax.fori_loop(0, 2, event, 0)


def last_kernel(flags, f, below, above, left, right, q, inverse, velocity, wide):
    def event(e, carry):
        for i in range(5):
            v = complete(lambda n: f[e, n], i, e, flags, below, above, left, right)
            for j in range(5):
                for k in range(5):
                    n = at(i, j, k)
                    wide[i, k, pl.ds(j, 8, stride=5), :] = q[e, n] + 0.5 * time_step * (v[j][k] * inverse[n])
            for k in range(5):
                velocity[e, i, :, k * 128 : (k + 1) * 128] = wide[i, k]
        return carry

    lax.fori_loop(0, 2, event, 0)


def correlate(d, forward, step, total, wide, tiles):
    def event(e, carry):
        def put(n, value):
            tiles[n] = value

        to_tiles(lambda i: forward[step, e, i].astype(f32), put, wide)

        def line(index):
            g = apply5(derivative, [d[e, n] for n in index])
            h = apply5(derivative, [tiles[n] for n in index])
            for a in range(5):
                total[index[a]] = total[index[a]] + g[a] * h[a]

        for_lines(line, directions)
        return carry

    lax.fori_loop(0, 2, event, 0)


def term_kernel(d1, d2, forward, wm, out, token, total, wide, tiles):
    def clear(n, carry):
        total[n] = jnp.zeros((8, 128), f32)
        return carry

    lax.fori_loop(0, points, clear, 0)
    correlate(d1, forward, 0, total, wide, tiles)
    correlate(d2, forward, 1, total, wide, tiles)
    token[...] = jnp.zeros_like(token)

    def tile(i, j, k):
        return total[at(i, j, k)] * wm[at(i, j, k)] * (-time_step / weight(i, j, k))

    def put_plane(i, k, rows):
        out[i, :, k * 128 : (k + 1) * 128] = rows

    from_tiles(tile, put_plane, wide)


def call(kernel, name, out_shapes, args, scratch=(), specs=None, outs=None, flops=10**6, moved=4 * 10**6, vmem=16, **more):
    return pl.pallas_call(
        kernel,
        name=name,
        out_shape=[s if hasattr(s, "dtype") else jax.ShapeDtypeStruct(s, f32) for s in out_shapes],
        in_specs=specs or [VMEM] * len(args),
        out_specs=outs or [VMEM] * len(out_shapes),
        scratch_shapes=list(scratch),
        compiler_params=pltpu.CompilerParams(vmem_limit_bytes=vmem * 2**20),
        cost_estimate=pl.CostEstimate(flops=flops, bytes_accessed=moved, transcendentals=0),
        **more,
    )(*args)


def swap(low, high, axis):
    count = lax.axis_size(axis)
    up = [(n, (n + 1) % count) for n in range(count)]
    down = [(b, a) for a, b in up]
    return lax.ppermute(high, axis, up), lax.ppermute(low, axis, down)


def on_device(d0, v0, modulus, density, forward, traces, owner, point):
    lat, lon = lax.axis_index("lat"), lax.axis_index("lon")
    lat_count, lon_count = lax.axis_size("lat"), lax.axis_size("lon")
    devices = lat_count * lon_count
    flags = [lat > 0, lat < lat_count - 1, lon > 0, lon < lon_count - 1, lon % 2 == 0]
    flags = jnp.stack(flags).astype(jnp.int32)
    field = (2, points, 8, 128)
    one = (points, 8, 128)
    wide_field = (2, padded, 8, 128)
    token = (8, 128)
    native = d0.shape
    d0, v0 = d0.reshape(2, 5, 40, 640), v0.reshape(2, 5, 40, 640)
    kernel_shape = modulus.shape
    modulus, density = modulus.reshape(5, 40, 640), density.reshape(5, 40, 640)
    forward = forward.reshape(2, 2, 5, 40, 640)
    receivers = owner.shape[0]

    def faces(channels):
        return [(channels, face_tiles, 8, 128)] * 2 + [(channels, 5, 8, 128)] * 2

    (packed,) = call(
        pack_kernel,
        "pack",
        [(2 * devices, 128)],
        (traces.transpose(1, 0, 2), owner.reshape(1, receivers), point.reshape(1, receivers)),
        [
            pltpu.VMEM((traces.shape[1], traces.shape[0], receivers), f32),
            pltpu.VMEM((1, receivers), jnp.int32),
            pltpu.VMEM((1, receivers), jnp.int32),
            pltpu.SemaphoreType.DMA((3,)),
        ],
        [HBM] * 3,
        vmem=56,
    )
    got = lax.all_to_all(packed.reshape(devices, 2, 128), ("lat", "lon"), 0, 0, tiled=True)
    got = got.reshape(2 * devices, 128)
    wide = pltpu.VMEM((5, 5, 40, 128), f32)
    tiles = pltpu.VMEM(one, f32)
    d, q, wm, mass, kept = call(
        start_kernel,
        "start",
        [field, field, one, one, (kept_tiles, 8, 128)],
        (d0, v0, modulus, density),
        [
            pltpu.VMEM(d0.shape, f32),
            pltpu.VMEM(v0.shape, f32),
            pltpu.VMEM(modulus.shape, bf16),
            pltpu.VMEM(density.shape, bf16),
        ]
        + [pltpu.VMEM(s, f32) for s in (field, field, one, one, field, (46, 8, 128))]
        + [wide, pltpu.SemaphoreType.DMA((16,))],
        [HBM] * 4,
        [HBM] * 5,
        flops=10**8,
        vmem=56,
    )
    scatter_scratch = [
        pltpu.VMEM((slots, devices), f32),
        pltpu.VMEM((slots, devices), f32),
        pltpu.VMEM((4, slots, devices), f32),
        pltpu.VMEM((1024, slots * devices), bf16),
        pltpu.VMEM((512, slots * devices), bf16),
    ]
    f, *edges = call(
        first_force_kernel,
        "first_force",
        [field] + faces(3),
        (got, kept),
        [pltpu.VMEM(field, f32), pltpu.SemaphoreType.DMA((6,))] + scatter_scratch,
        [VMEM, HBM],
        flops=4 * 10**9,
        vmem=18,
    )

    def source(step, order):
        return call(
            functools.partial(source_kernel, step),
            "source",
            [wide_field, token],
            (got, order),
            scatter_scratch,
            [VMEM, ANY],
            flops=4 * 10**9,
            vmem=18,
        )

    def exchange(edges, order):
        face_low, face_high, row_low, row_high = edges
        below, above = swap(face_low, face_high, "lat")
        even, odd = call(
            rows_kernel,
            "rows",
            [row_low.shape] * 2,
            (flags, below, above, row_low, row_high, order),
            specs=[SMEM] + [VMEM] * 4 + [ANY],
            moved=4 * 10**5,
            vmem=4,
        )
        pairs = [(n, n ^ 1) for n in range(lon_count)]
        between = [(n, (n + 1 if n % 2 else n - 1) % lon_count) for n in range(lon_count)]
        return below, above, lax.ppermute(even, "lon", pairs), lax.ppermute(odd, "lon", between)

    specs = [SMEM] + [VMEM] * 10
    s1, order = source(1, edges[2])
    received = exchange(edges, order)
    d1, q, inverse, f, *edges = call(
        functools.partial(step_kernel, True),
        "first_step",
        [field, field, one, field] + faces(2),
        (flags, f, *received, d, q, s1, wm, mass),
        specs=specs,
        flops=10**8,
    )
    s2, order = source(2, edges[2])
    received = exchange(edges, order)
    d2, q, f, *edges = call(
        functools.partial(step_kernel, False),
        "second_step",
        [field, field, field] + faces(2),
        (flags, f, *received, d1, q, s2, wm, inverse),
        specs=specs,
        flops=10**8,
    )
    kernel, order = call(
        term_kernel, "term", [(5, 40, 640), token], (d1, d2, forward, wm), [tiles, wide, tiles], flops=10**8
    )
    received = exchange(edges, order)
    (velocity,) = call(
        last_kernel, "last", [(2, 5, 40, 640)], (flags, f, *received, q, inverse), [wide], [SMEM] + [VMEM] * 7
    )
    return velocity.reshape(native), kernel.reshape(kernel_shape)


def solution(mesh):
    placed = (
        P(None, "lat", None, "lon", None),
        P(None, "lat", None, "lon", None),
        P("lat", None, "lon", None),
        P("lat", None, "lon", None),
        P(None, None, "lat", None, "lon", None),
        P(None, None, ("lat", "lon")),
        P(("lat", "lon")),
        P(("lat", "lon")),
    )
    return jax.shard_map(
        on_device,
        mesh=mesh,
        in_specs=placed,
        out_specs=(P(None, "lat", None, "lon", None), P("lat", None, "lon", None)),
        check_vma=False,
    )
```

```python
import functools
import math

import jax
import jax.numpy as jnp
import numpy as np
from jax import lax
from jax.experimental import pallas as pl
from jax.experimental.pallas import tpu as pltpu
from jax.sharding import PartitionSpec as P

time_step = 0.05
f32 = jnp.float32
bf16 = jnp.bfloat16
points = 125
padded = 128
slots = 32
face_tiles = 18
kept_tiles = 12288
VMEM = pl.BlockSpec(memory_space=pltpu.VMEM)
SMEM = pl.BlockSpec(memory_space=pltpu.SMEM)
HBM = pl.BlockSpec(memory_space=pltpu.HBM)
ANY = pl.BlockSpec(memory_space=pl.ANY)


def gll_tables():
    root_value = math.sqrt(3.0 / 7.0)
    gll_points = np.array([-1.0, -root_value, 0.0, root_value, 1.0])
    gll_weights = np.array([0.1, 49.0 / 90.0, 32.0 / 45.0, 49.0 / 90.0, 0.1])
    legendre = (35.0 * gll_points**4 - 30.0 * gll_points**2 + 3.0) / 8.0
    derivative = np.zeros((5, 5))
    for a in range(5):
        for b in range(5):
            if a != b:
                derivative[a, b] = legendre[a] / legendre[b] / (gll_points[a] - gll_points[b])
    derivative[0, 0] = -5.0
    derivative[4, 4] = 5.0
    return derivative, gll_weights


derivative, gll_weights = gll_tables()
transposed = derivative.T


def weight(i, j, k):
    return float(gll_weights[i] * gll_weights[j] * gll_weights[k])


def apply5(matrix, u):
    odd = (u[0] - u[4], u[1] - u[3])
    even = (u[0] + u[4], u[1] + u[3])
    out = [None] * 5
    for a in (0, 1):
        p = float(0.5 * (matrix[a, 0] - matrix[a, 4])) * odd[0]
        p = p + float(0.5 * (matrix[a, 1] - matrix[a, 3])) * odd[1]
        m = float(0.5 * (matrix[a, 0] + matrix[a, 4])) * even[0]
        m = m + float(0.5 * (matrix[a, 1] + matrix[a, 3])) * even[1]
        m = m + float(matrix[a, 2]) * u[2]
        out[a] = p + m
        out[4 - a] = p - m
    out[2] = float(matrix[2, 0]) * odd[0] + float(matrix[2, 1]) * odd[1]
    return out


directions = ((5, 1, 25), (25, 1, 5), (25, 5, 1))


def for_lines(body, directions):
    for outer, inner, step in directions:
        for t in range(5):
            for line in range(5):
                base = t * outer + line * inner
                body([base + step * n for n in range(5)])


def sublane():
    return lax.broadcasted_iota(jnp.int32, (8, 128), 0)


def lane():
    return lax.broadcasted_iota(jnp.int32, (8, 128), 1)


def row_of(tile, index):
    return jnp.broadcast_to(tile[index : index + 1, :], (8, 128))


def column_of(tile, index):
    return jnp.broadcast_to(tile[:, index : index + 1], (8, 128))


def at(i, j, k):
    return (i * 5 + j) * 5 + k


def to_tiles(plane, put, wide):
    for i in range(5):
        rows = plane(i)
        for k in range(5):
            wide[i, k] = rows[:, k * 128 : (k + 1) * 128]
        for j in range(5):
            for k in range(5):
                put(at(i, j, k), wide[i, k, pl.ds(j, 8, stride=5), :])


def from_tiles(tile, put_plane, wide):
    for i in range(5):
        for j in range(5):
            for k in range(5):
                wide[i, k, pl.ds(j, 8, stride=5), :] = tile(i, j, k)
        for k in range(5):
            put_plane(i, k, wide[i, k])


def force(d, f, e, wm, source):
    def line(index, before):
        g = apply5(derivative, [d[e, n] for n in index])
        r = apply5(transposed, [g[a] * wm[index[a]] for a in range(5)])
        for a in range(5):
            f[e, index[a]] = before(index[a]) - r[a]

    for_lines(lambda index: line(index, source), directions[:1])
    for_lines(lambda index: line(index, lambda n: f[e, n]), directions[1:])


def fold(get, put, every=False):
    sub, ln = sublane(), lane()
    for i in range(5):
        v = [[get(at(i, j, k)) for k in range(5)] for j in range(5)]
        for k in range(5):
            v[0][k] = v[0][k] + jnp.where(sub == 0, 0.0, pltpu.roll(v[4][k], 1, 0))
        for j in range(5):
            v[j][0] = v[j][0] + jnp.where(ln == 0, 0.0, pltpu.roll(v[j][4], 1, 1))
        for j in range(5):
            for k in range(5):
                if every or j == 0 or k == 0:
                    put(at(i, j, k), v[j][k])


def emit_faces(get, c, face_low, face_high, row_low=None, row_high=None):
    lead = () if c is None else (c,)
    sub, ln = sublane(), lane()
    for i, face in ((0, face_low), (4, face_high)):
        last_row = jnp.zeros((8, 128), f32)
        last_column = jnp.zeros((8, 128), f32)
        for k in range(5):
            last_row = jnp.where(sub == k, row_of(get(at(i, 4, k)), 7), last_row)
        for j in range(4):
            last_column = jnp.where(ln == j, column_of(get(at(i, j, 4)), 127), last_column)
            for k in range(4):
                face[lead + (j * 4 + k,)] = get(at(i, j, k))
        face[lead + (16,)] = last_row
        face[lead + (17,)] = last_column
    for i in range(5) if row_low is not None else ():
        low = jnp.zeros((8, 128), f32)
        high = jnp.zeros((8, 128), f32)
        for k in range(5):
            low = jnp.where(sub == k, row_of(get(at(i, 0, k)), 0), low)
            high = jnp.where(sub == k, row_of(get(at(i, 4, k)), 7), high)
        row_low[lead + (i,)] = low
        row_high[lead + (i,)] = high


def complete(get, i, c, flags, from_below, from_above, left=None, right=None):
    sub, ln = sublane(), lane()
    v = [[get(at(i, j, k)) for k in range(5)] for j in range(5)]
    if i in (0, 4):
        face = from_below if i == 0 else from_above
        keep = flags[0 if i == 0 else 1] > 0
        for j in range(4):
            for k in range(4):
                v[j][k] = v[j][k] + jnp.where(keep, face[c, j * 4 + k], 0.0)
        last_row, last_column = face[c, 16], face[c, 17]
        for k in range(5):
            v[4][k] = v[4][k] + jnp.where((sub == 7) & keep, row_of(last_row, k), 0.0)
        for j in range(4):
            v[j][4] = v[j][4] + jnp.where((ln == 127) & keep, column_of(last_column, j), 0.0)
    if left is not None:
        for k in range(5):
            v[0][k] = v[0][k] + jnp.where((sub == 0) & (flags[2] > 0), row_of(left, k), 0.0)
            v[4][k] = v[4][k] + jnp.where((sub == 7) & (flags[3] > 0), row_of(right, k), 0.0)
    for k in range(5):
        v[4][k] = jnp.where(sub == 7, v[4][k], pltpu.roll(v[0][k], 7, 0))
    for j in range(5):
        v[j][4] = jnp.where(ln == 127, v[j][4], pltpu.roll(v[j][0], 127, 1))
    return v


def sides(flags, from_even, from_odd, *index):
    even, odd = from_even[index], from_odd[index]
    return jnp.where(flags[4] > 0, odd, even), jnp.where(flags[4] > 0, even, odd)


def send_sides(flags, even_out, odd_out, index, low, high):
    even_out[index] = jnp.where(flags[4] > 0, high, low)
    odd_out[index] = jnp.where(flags[4] > 0, low, high)


def stack_rows(rows, first=0, tile=None):
    sub = sublane()
    tile = jnp.zeros((8, 128), f32) if tile is None else tile
    for n, (source, index) in enumerate(rows):
        tile = jnp.where(sub == first + n, row_of(source, index), tile)
    return tile


def pack_kernel(traces_in, owner_in, point_in, out, traces, owner, point, sems):
    pairs = ((traces_in, traces), (owner_in, owner), (point_in, point))
    copies = [pltpu.make_async_copy(a, b, sems.at[n]) for n, (a, b) in enumerate(pairs)]
    for copy in copies:
        copy.start()
    for copy in copies:
        copy.wait()
    devices = out.shape[0] // 2
    receivers = owner.shape[1]
    p = point[...]
    hi = p >> 7
    lo = p & 127

    def divide(x, by):
        return jnp.floor((x.astype(f32) + 0.5) * (1.0 / by)).astype(jnp.int32)

    t = divide(hi, 5)
    k = hi - 5 * t
    i = divide(t, 40)
    row = t - 40 * i
    ey = divide(row, 5)
    j = row - 5 * ey
    place = ((((i * 5 + j) * 5 + k) * 8 + ey) * 128 + lo).astype(f32)
    rows = [traces[0, 0:1, :], traces[0, 1:2, :], place, traces[1, 0:1, :]]
    rows += [traces[1, 1:2, :], traces[2, 0:1, :], traces[2, 1:2, :], jnp.zeros((1, receivers), f32)]
    owned = lax.broadcasted_iota(jnp.int32, (devices, receivers), 0) == owner[...]
    owned = jnp.where(owned, 1.0, 0.0)
    before = lax.broadcasted_iota(jnp.int32, (128, 128), 0) < lax.broadcasted_iota(jnp.int32, (128, 128), 1)
    before = jnp.where(before, 1.0, 0.0).astype(bf16)
    carry = jnp.zeros((devices, 1), f32)
    ranks = []
    for chunk in range(receivers // 128):
        part = owned[:, chunk * 128 : (chunk + 1) * 128]
        earlier = jnp.dot(part.astype(bf16), before, preferred_element_type=f32) + carry
        ranks.append(jnp.sum(part * earlier, axis=0, keepdims=True))
        carry = carry + jnp.sum(part, axis=1, keepdims=True)
    rank = jnp.concatenate(ranks, axis=1).astype(jnp.int32)
    chosen = lax.broadcasted_iota(jnp.int32, (slots, receivers), 0) == rank
    owned = owned.astype(bf16)
    total = jnp.zeros((devices, 256), f32)
    left = rows
    for _ in range(3):
        pieces = [v.astype(bf16) for v in left]
        left = [v - q.astype(f32) for v, q in zip(left, pieces)]
        table = jnp.concatenate([jnp.where(chosen, q.astype(f32), 0.0) for q in pieces], axis=0)
        total = total + lax.dot_general(
            owned, table.astype(bf16), (((1,), (1,)), ((), ())), preferred_element_type=f32
        )
    out[pl.ds(0, devices, stride=2), :] = total[:, :128]
    out[pl.ds(1, devices, stride=2), :] = total[:, 128:]


def scatter(places, values, hi_rows, lo_rows, piece_rows, left_side, right_side, store):
    place = places.astype(jnp.int32)
    hi_rows[...] = (place >> 7).astype(f32)
    lo_rows[...] = (place & 127).astype(f32)
    count = len(values)
    for c, v in enumerate(values):
        upper = v.astype(bf16).astype(f32)
        piece_rows[2 * c] = upper
        piece_rows[2 * c + 1] = v - upper
    index = [lax.broadcasted_iota(jnp.int32, (16, 128), 0).astype(f32) + 16.0 * g for g in range(8)]
    index = [x.astype(bf16) for x in index]
    one, zero = jnp.ones((16, 128), bf16), jnp.zeros((16, 128), bf16)

    def fill_right(r):
        where = slice(r * 128, r * 128 + 128)
        lo = jnp.broadcast_to(lo_rows[r : r + 1, :], (16, 128)).astype(bf16)
        pieces = [jnp.broadcast_to(piece_rows[n, r : r + 1, :], (16, 128)).astype(bf16) for n in range(2 * count)]
        for g in range(8):
            same = index[g] == lo
            for n in range(2 * count):
                at_row = n * 128 + g * 16
                right_side[at_row : at_row + 16, where] = jnp.where(same, pieces[n], zero)

    def fill_left(r, m):
        where = slice(r * 128, r * 128 + 128)
        hi = jnp.broadcast_to(hi_rows[r : r + 1, :], (16, 128))
        part = (hi - 128.0 * m).astype(bf16)
        for g in range(8):
            left_side[m * 128 + g * 16 : m * 128 + g * 16 + 16, where] = jnp.where(index[g] == part, one, zero)

    def fill_tile(m):
        for r in range(slots):
            fill_left(r, 2 * m)
            fill_left(r, 2 * m + 1)

    for r in range(slots):
        fill_right(r)
    fill_tile(0)
    for m in range(4):
        if m < 3:
            fill_tile(m + 1)
        for c in range(count):
            both = lax.dot_general(
                left_side[m * 256 : m * 256 + 256, :],
                right_side[c * 256 : c * 256 + 256, :],
                (((1,), (1,)), ((), ())),
                preferred_element_type=f32,
            )
            store(c, m, both[:, :128] + both[:, 128:])


def start_kernel(d_in, v_in, k_in, m_in, d_out, v_out, wm_out, mass_out, rim_out, kept, *scratch):
    d0, v0, modulus, density, d, v, wm, mass, rim, kd, edges, wide, sems = scratch
    copies = []

    def copy(source, target):
        copies.append(pltpu.make_async_copy(source, target, sems.at[len(copies)]))
        copies[-1].start()
        return copies[-1]

    loads = [copy(k_in, modulus), copy(d_in.at[0], d0.at[0]), copy(d_in.at[1], d0.at[1])]
    loads += [copy(m_in, density), copy(v_in, v0)]

    def weighted(target):
        def put(n, value):
            target[n] = value * weight(n // 25, n // 5 % 5, n % 5)

        return put

    loads[0].wait()
    to_tiles(lambda i: modulus[i].astype(f32), weighted(wm), wide)
    copy(wm, wm_out)
    for i in range(5):
        for j in range(5):
            tiles = [wm[at(i, j, k)] for k in range(5)]
            rim[0, i * 5 + j] = stack_rows([(tile, 0) for tile in tiles])
            rim[1, i * 5 + j] = stack_rows([(tile, 7) for tile in tiles])
    copy(rim, rim_out)
    for e in range(2):

        def put_d(n, value, e=e):
            d[e, n] = value

        loads[1 + e].wait()
        to_tiles(lambda i, e=e: d0[e, i], put_d, wide)
        copy(d.at[e], d_out.at[e])
        force(d, kd, e, wm, lambda n: 0.0)
        copy(kd.at[e], kept.at[e * points : e * points + points])
    loads[3].wait()
    to_tiles(lambda i: density[i].astype(f32), weighted(mass), wide)

    def put_mass(n, value):
        mass[n] = value

    fold(lambda n: mass[n], put_mass)
    copy(mass, mass_out)
    low, high, row_low, row_high = edges.at[0:18], edges.at[18:36], edges.at[36:41], edges.at[41:46]
    emit_faces(lambda n: mass[n], None, low, high, row_low, row_high)
    copy(edges, kept.at[2 * points : 2 * points + 46])
    loads[4].wait()
    for e in range(2):

        def put_v(n, value, e=e):
            v[e, n] = value

        to_tiles(lambda i, e=e: v0[e, i], put_v, wide)
        copy(v.at[e], v_out.at[e])
    for pending in copies[len(loads) :]:
        pending.wait()


def first_force_kernel(got, kept, f, face_low, face_high, row_low, row_high, kd, sems, *scratch):
    edges = kept.at[2 * points : 2 * points + 46]
    pairs = ((kept.at[0:points], kd.at[0]), (kept.at[points : 2 * points], kd.at[1]))
    pairs += ((edges.at[0:18], face_low.at[2]), (edges.at[18:36], face_high.at[2]))
    pairs += ((edges.at[36:41], row_low.at[2]), (edges.at[41:46], row_high.at[2]))
    copies = [pltpu.make_async_copy(a, b, sems.at[n]) for n, (a, b) in enumerate(pairs)]
    for copy in copies:
        copy.start()
    devices = got.shape[0] // 2
    first = got[pl.ds(0, devices, stride=2), :].T

    def store(c, m, value):
        count = min(32, points - 32 * m)
        f[c, 32 * m : 32 * m + count] = value.reshape(32, 8, 128)[:count]

    scatter(first[64:96], [first[0:32], first[32:64]], *scratch, store)
    for copy in copies:
        copy.wait()

    def event(e, carry):
        def put(n, value):
            f[e, n] = value

        fold(lambda n: f[e, n] + kd[e, n], put, every=True)
        emit_faces(lambda n: f[e, n], e, face_low, face_high, row_low, row_high)
        return carry

    lax.fori_loop(0, 2, event, 0)


def source_kernel(step, got, order, s, token, *scratch):
    devices = got.shape[0] // 2
    first = got[pl.ds(0, devices, stride=2), :].T
    second = got[pl.ds(1, devices, stride=2), :].T
    token[...] = jnp.zeros_like(token)

    def store(c, m, value):
        s[c, 32 * m : 32 * m + 32] = value.reshape(32, 8, 128)

    values = [first[96:128], second[0:32]] if step == 1 else [second[32:64], second[64:96]]
    scatter(first[64:96], values, *scratch, store)


def rows_kernel(flags, from_below, from_above, row_low, row_high, wm_rim, order, even_out, odd_out):
    sub, ln = sublane(), lane()
    for c in range(row_low.shape[0]):
        for i in range(5):
            low, high = row_low[c, i], row_high[c, i]
            if i in (0, 4):
                face = from_below if i == 0 else from_above
                keep = flags[0 if i == 0 else 1] > 0
                extra = stack_rows([(face[c, k], 0) for k in range(4)])
                corner = jnp.broadcast_to(face[c, 17][0:1, 0:1], (8, 128))
                extra = jnp.where((sub == 4) & (ln == 127), corner, extra)
                low = low + jnp.where(keep, extra, 0.0)
                high = high + jnp.where(keep, face[c, 16], 0.0)
            send_sides(flags, even_out, odd_out, c * 5 + i, low, high)
    for n in range(25):
        send_sides(flags, even_out, odd_out, 15 + n, wm_rim[0, n], wm_rim[1, n])


def first_step_kernel(flags, f, below, above, even, odd, d, q, source, wm, mass, *refs):
    d_out, q_out, inverse, f_out, face_low, face_high = refs
    for i in range(5):
        v = complete(lambda n: mass[n], i, 2, flags, below, above, *sides(flags, even, odd, 10 + i))
        for j in range(5):
            for k in range(5):
                inverse[at(i, j, k)] = 1.0 / v[j][k]

    def event(e, carry):
        for i in range(5):
            v = complete(lambda n: f[e, n], i, e, flags, below, above, *sides(flags, even, odd, e * 5 + i))
            for j in range(5):
                for k in range(5):
                    n = at(i, j, k)
                    q_new = q[e, n] + 0.5 * time_step * (v[j][k] * inverse[n])
                    q_out[e, n] = q_new
                    d_out[e, n] = d[e, n] + time_step * q_new
        force(d_out, f_out, e, wm, lambda n: source[e, n])

        def put(n, value):
            f_out[e, n] = value

        fold(lambda n: f_out[e, n], put)
        emit_faces(lambda n: f_out[e, n], e, face_low, face_high)
        return carry

    lax.fori_loop(0, 2, event, 0)


def advance_kernel(flags, f, below, above, d, q, inverse, source, d_out, q_out, even_out, odd_out):
    def event(e, carry):
        for i in range(5):
            v = complete(lambda n: f[e, n], i, e, flags, below, above)
            new = [[None] * 5 for _ in range(5)]
            for j in range(5):
                for k in range(5):
                    n = at(i, j, k)
                    q_new = q[e, n] + time_step * (v[j][k] * inverse[n])
                    q_out[e, n] = q_new
                    new[j][k] = d[e, n] + time_step * q_new
                    d_out[e, n] = new[j][k]
            for m in range(4):
                low = stack_rows([(new[m + 1][k], 0) for k in range(5)])
                high = stack_rows([(new[m][k], 7) for k in range(5)])
                which = range(3) if m % 2 == 0 else range(3, 5)
                if m < 2:
                    low = stack_rows([(v[0][k], 0) for k in which], 5, low)
                    high = stack_rows([(v[4][k], 7) for k in which], 5, high)
                else:
                    low = stack_rows([(source[e, at(i, 0, k)], 0) for k in which], 5, low)
                    high = stack_rows([(source[e, at(i, 4, k)], 7) for k in which], 5, high)
                send_sides(flags, even_out, odd_out, (e, i * 4 + m), low, high)
        return carry

    lax.fori_loop(0, 2, event, 0)


def along_sublanes(matrix, tile):
    sub = sublane()
    total = None
    for n in range(5):
        weights = jnp.zeros((8, 128), f32)
        for m in range(5):
            weights = jnp.where(sub == m, float(matrix[m, n]), weights)
        term = weights * row_of(tile, n)
        total = term if total is None else total + term
    return total


def rim_force(u, wm, near):
    out = []
    gx = apply5(derivative, [u[i][near] for i in range(5)])
    rx = apply5(transposed, [gx[i] * wm[i][near] for i in range(5)])
    for i in range(5):
        gy = apply5(derivative, u[i])
        ry = apply5(transposed, [gy[j] * wm[i][j] for j in range(5)])[near]
        gz = along_sublanes(derivative, u[i][near])
        rz = along_sublanes(transposed, gz * wm[i][near])
        out.append(rx[i] + ry + rz)
    return out


def second_step_kernel(flags, even, odd, wm_even, wm_odd, d, q, inverse, source, wm, *refs):
    d_out, q_out, f_out, face_low, face_high = refs
    sub = sublane()

    def event(e, carry):
        for i in range(5):
            message = [sides(flags, even, odd, e, i * 4 + m) for m in range(4)]
            for j in range(5):
                for k in range(5):
                    n = at(i, j, k)
                    d_new, q_new = d[e, n], q[e, n]
                    if j in (0, 4):
                        side = 0 if j == 0 else 1
                        row = row_of(message[0][side], 5 + k) if k < 3 else row_of(message[1][side], 2 + k)
                        mine = (sub == (0 if j == 0 else 7)) & (flags[2 + side] > 0)
                        change = time_step * (jnp.where(mine, row, 0.0) * inverse[n])
                        q_new = q_new + change
                        d_new = d_new + time_step * change
                    d_out[e, n] = d_new
                    q_out[e, n] = q_new
        force(d_out, f_out, e, wm, lambda n: source[e, n])
        for side in range(2):
            j, edge = (0, 0) if side == 0 else (4, 7)
            near = 4 - j
            u, w, message = [], [], []
            for i in range(5):
                message.append([sides(flags, even, odd, e, i * 4 + m)[side] for m in range(4)])
                shared = stack_rows([(d_out[e, at(i, j, k)], edge) for k in range(5)])
                u.append(message[i] + [shared] if near == 4 else [shared] + message[i])
                w.append([sides(flags, wm_even, wm_odd, 15 + i * 5 + m)[side] for m in range(5)])
            r = rim_force(u, w, near)
            mine = (sub == edge) & (flags[2 + side] > 0)
            for i in range(5):
                for k in range(5):
                    row = row_of(message[i][2], 5 + k) if k < 3 else row_of(message[i][3], 2 + k)
                    n = at(i, j, k)
                    f_out[e, n] = f_out[e, n] + jnp.where(mine, row - row_of(r[i], k), 0.0)

        def put(n, value):
            f_out[e, n] = value

        fold(lambda n: f_out[e, n], put)
        emit_faces(lambda n: f_out[e, n], e, face_low, face_high)
        return carry

    lax.fori_loop(0, 2, event, 0)


def last_kernel(flags, f, below, above, q, inverse, order, velocity, wide):
    def event(e, carry):
        for i in range(5):
            v = complete(lambda n: f[e, n], i, e, flags, below, above)
            for j in range(5):
                for k in range(5):
                    n = at(i, j, k)
                    wide[i, k, pl.ds(j, 8, stride=5), :] = q[e, n] + 0.5 * time_step * (v[j][k] * inverse[n])
            for k in range(5):
                velocity[e, i, :, k * 128 : (k + 1) * 128] = wide[i, k]
        return carry

    lax.fori_loop(0, 2, event, 0)


def correlate(d, forward, step, total, wide, tiles):
    def event(e, carry):
        def put(n, value):
            tiles[n] = value

        to_tiles(lambda i: forward[step, e, i].astype(f32), put, wide)

        def line(index):
            g = apply5(derivative, [d[e, n] for n in index])
            h = apply5(derivative, [tiles[n] for n in index])
            for a in range(5):
                total[index[a]] = total[index[a]] + g[a] * h[a]

        for_lines(line, directions)
        return carry

    lax.fori_loop(0, 2, event, 0)


def term_kernel(d1, d2, forward, wm, out, token, total, wide, tiles):
    def clear(n, carry):
        total[n] = jnp.zeros((8, 128), f32)
        return carry

    lax.fori_loop(0, points, clear, 0)
    correlate(d1, forward, 0, total, wide, tiles)
    correlate(d2, forward, 1, total, wide, tiles)
    token[...] = jnp.zeros_like(token)

    def tile(i, j, k):
        return total[at(i, j, k)] * wm[at(i, j, k)] * (-time_step / weight(i, j, k))

    def put_plane(i, k, rows):
        out[i, :, k * 128 : (k + 1) * 128] = rows

    from_tiles(tile, put_plane, wide)


def call(kernel, name, out_shapes, args, scratch=(), specs=None, outs=None, flops=10**6, moved=4 * 10**6, vmem=16, **more):
    return pl.pallas_call(
        kernel,
        name=name,
        out_shape=[s if hasattr(s, "dtype") else jax.ShapeDtypeStruct(s, f32) for s in out_shapes],
        in_specs=specs or [VMEM] * len(args),
        out_specs=outs or [VMEM] * len(out_shapes),
        scratch_shapes=list(scratch),
        compiler_params=pltpu.CompilerParams(vmem_limit_bytes=vmem * 2**20),
        cost_estimate=pl.CostEstimate(flops=flops, bytes_accessed=moved, transcendentals=0),
        **more,
    )(*args)


def swap(low, high, axis):
    count = lax.axis_size(axis)
    up = [(n, (n + 1) % count) for n in range(count)]
    down = [(b, a) for a, b in up]
    return lax.ppermute(high, axis, up), lax.ppermute(low, axis, down)


def on_device(d0, v0, modulus, density, forward, traces, owner, point):
    lat, lon = lax.axis_index("lat"), lax.axis_index("lon")
    lat_count, lon_count = lax.axis_size("lat"), lax.axis_size("lon")
    devices = lat_count * lon_count
    flags = [lat > 0, lat < lat_count - 1, lon > 0, lon < lon_count - 1, lon % 2 == 0]
    flags = jnp.stack(flags).astype(jnp.int32)
    field = (2, points, 8, 128)
    one = (points, 8, 128)
    wide_field = (2, padded, 8, 128)
    token = (8, 128)
    native = d0.shape
    d0, v0 = d0.reshape(2, 5, 40, 640), v0.reshape(2, 5, 40, 640)
    kernel_shape = modulus.shape
    modulus, density = modulus.reshape(5, 40, 640), density.reshape(5, 40, 640)
    forward = forward.reshape(2, 2, 5, 40, 640)
    receivers = owner.shape[0]

    def faces(channels):
        return [(channels, face_tiles, 8, 128)] * 2

    (packed,) = call(
        pack_kernel,
        "pack",
        [(2 * devices, 128)],
        (traces.transpose(1, 0, 2), owner.reshape(1, receivers), point.reshape(1, receivers)),
        [
            pltpu.VMEM((traces.shape[1], traces.shape[0], receivers), f32),
            pltpu.VMEM((1, receivers), jnp.int32),
            pltpu.VMEM((1, receivers), jnp.int32),
            pltpu.SemaphoreType.DMA((3,)),
        ],
        [HBM] * 3,
        vmem=56,
    )
    got = lax.all_to_all(packed.reshape(devices, 2, 128), ("lat", "lon"), 0, 0, tiled=True)
    got = got.reshape(2 * devices, 128)
    wide = pltpu.VMEM((5, 5, 40, 128), f32)
    tiles = pltpu.VMEM(one, f32)
    rim = (2, 25, 8, 128)
    d, q, wm, mass, wm_rim, kept = call(
        start_kernel,
        "start",
        [field, field, one, one, rim, (kept_tiles, 8, 128)],
        (d0, v0, modulus, density),
        [
            pltpu.VMEM(d0.shape, f32),
            pltpu.VMEM(v0.shape, f32),
            pltpu.VMEM(modulus.shape, bf16),
            pltpu.VMEM(density.shape, bf16),
        ]
        + [pltpu.VMEM(s, f32) for s in (field, field, one, one, rim, field, (46, 8, 128))]
        + [wide, pltpu.SemaphoreType.DMA((16,))],
        [HBM] * 4,
        [HBM] * 6,
        flops=10**8,
        vmem=56,
    )
    scatter_scratch = [
        pltpu.VMEM((slots, devices), f32),
        pltpu.VMEM((slots, devices), f32),
        pltpu.VMEM((4, slots, devices), f32),
        pltpu.VMEM((1024, slots * devices), bf16),
        pltpu.VMEM((512, slots * devices), bf16),
    ]
    f, *edges = call(
        first_force_kernel,
        "first_force",
        [field] + faces(3) + [(3, 5, 8, 128)] * 2,
        (got, kept),
        [pltpu.VMEM(field, f32), pltpu.SemaphoreType.DMA((6,))] + scatter_scratch,
        [VMEM, HBM],
        flops=4 * 10**9,
        vmem=18,
    )

    def source(step, order):
        return call(
            functools.partial(source_kernel, step),
            "source",
            [wide_field, token],
            (got, order),
            scatter_scratch,
            [VMEM, ANY],
            flops=4 * 10**9,
            vmem=18,
        )

    def trade(even, odd):
        pairs = [(n, n ^ 1) for n in range(lon_count)]
        between = [(n, (n + 1 if n % 2 else n - 1) % lon_count) for n in range(lon_count)]
        return lax.ppermute(even, "lon", pairs), lax.ppermute(odd, "lon", between)

    face_low, face_high, row_low, row_high = edges
    s1, order = source(1, row_low)
    beside = swap(face_low, face_high, "lat")
    first_message = call(
        rows_kernel,
        "rows",
        [(40, 8, 128)] * 2,
        (flags, *beside, row_low, row_high, wm_rim, order),
        specs=[SMEM] + [VMEM] * 5 + [ANY],
        moved=4 * 10**5,
        vmem=4,
    )
    first_message = trade(*first_message)
    d1, q, inverse, f, *edges = call(
        first_step_kernel,
        "first_step",
        [field, field, one, field] + faces(2),
        (flags, f, *beside, *first_message, d, q, s1, wm, mass),
        specs=[SMEM] + [VMEM] * 10,
        flops=10**8,
    )
    s2, unused = source(2, edges[0])
    beside = swap(*edges, "lat")
    d2, q, *second_message = call(
        advance_kernel,
        "advance",
        [field, field] + [(2, 20, 8, 128)] * 2,
        (flags, f, *beside, d1, q, inverse, s2),
        specs=[SMEM] + [VMEM] * 7,
        flops=10**7,
    )
    second_message = trade(*second_message)
    d2, q, f, *edges = call(
        second_step_kernel,
        "second_step",
        [field, field, field] + faces(2),
        (flags, *second_message, *first_message, d2, q, inverse, s2, wm),
        specs=[SMEM] + [VMEM] * 9,
        flops=10**8,
    )
    kernel, order = call(
        term_kernel, "term", [(5, 40, 640), token], (d1, d2, forward, wm), [tiles, wide, tiles], flops=10**8
    )
    beside = swap(*edges, "lat")
    (velocity,) = call(
        last_kernel,
        "last",
        [(2, 5, 40, 640)],
        (flags, f, *beside, q, inverse, order),
        [wide],
        [SMEM] + [VMEM] * 5 + [ANY],
    )
    return velocity.reshape(native), kernel.reshape(kernel_shape)


def solution(mesh):
    placed = (
        P(None, "lat", None, "lon", None),
        P(None, "lat", None, "lon", None),
        P("lat", None, "lon", None),
        P("lat", None, "lon", None),
        P(None, None, "lat", None, "lon", None),
        P(None, None, ("lat", "lon")),
        P(("lat", "lon")),
        P(("lat", "lon")),
    )
    return jax.shard_map(
        on_device,
        mesh=mesh,
        in_specs=placed,
        out_specs=(P(None, "lat", None, "lon", None), P("lat", None, "lon", None)),
        check_vma=False,
    )
```

```python
import functools
import math

import jax
import jax.numpy as jnp
import numpy as np
from jax import lax
from jax.experimental import pallas as pl
from jax.experimental.pallas import tpu as pltpu
from jax.sharding import PartitionSpec as P

time_step = 0.05
f32 = jnp.float32
bf16 = jnp.bfloat16
points = 125
padded = 128
slots = 32
face_tiles = 18
kept_tiles = 12288
VMEM = pl.BlockSpec(memory_space=pltpu.VMEM)
SMEM = pl.BlockSpec(memory_space=pltpu.SMEM)
HBM = pl.BlockSpec(memory_space=pltpu.HBM)
ANY = pl.BlockSpec(memory_space=pl.ANY)


def gll_tables():
    root_value = math.sqrt(3.0 / 7.0)
    gll_points = np.array([-1.0, -root_value, 0.0, root_value, 1.0])
    gll_weights = np.array([0.1, 49.0 / 90.0, 32.0 / 45.0, 49.0 / 90.0, 0.1])
    legendre = (35.0 * gll_points**4 - 30.0 * gll_points**2 + 3.0) / 8.0
    derivative = np.zeros((5, 5))
    for a in range(5):
        for b in range(5):
            if a != b:
                derivative[a, b] = legendre[a] / legendre[b] / (gll_points[a] - gll_points[b])
    derivative[0, 0] = -5.0
    derivative[4, 4] = 5.0
    return derivative, gll_weights


derivative, gll_weights = gll_tables()
transposed = derivative.T


def weight(i, j, k):
    return float(gll_weights[i] * gll_weights[j] * gll_weights[k])


def apply5(matrix, u):
    odd = (u[0] - u[4], u[1] - u[3])
    even = (u[0] + u[4], u[1] + u[3])
    out = [None] * 5
    for a in (0, 1):
        p = float(0.5 * (matrix[a, 0] - matrix[a, 4])) * odd[0]
        p = p + float(0.5 * (matrix[a, 1] - matrix[a, 3])) * odd[1]
        m = float(0.5 * (matrix[a, 0] + matrix[a, 4])) * even[0]
        m = m + float(0.5 * (matrix[a, 1] + matrix[a, 3])) * even[1]
        m = m + float(matrix[a, 2]) * u[2]
        out[a] = p + m
        out[4 - a] = p - m
    out[2] = float(matrix[2, 0]) * odd[0] + float(matrix[2, 1]) * odd[1]
    return out


directions = ((5, 1, 25), (25, 1, 5), (25, 5, 1))


def for_lines(body, directions):
    for outer, inner, step in directions:
        for t in range(5):
            for line in range(5):
                base = t * outer + line * inner
                body([base + step * n for n in range(5)])


def sublane():
    return lax.broadcasted_iota(jnp.int32, (8, 128), 0)


def lane():
    return lax.broadcasted_iota(jnp.int32, (8, 128), 1)


def row_of(tile, index):
    return jnp.broadcast_to(tile[index : index + 1, :], (8, 128))


def column_of(tile, index):
    return jnp.broadcast_to(tile[:, index : index + 1], (8, 128))


def at(i, j, k):
    return (i * 5 + j) * 5 + k


def to_tiles(plane, put, wide):
    for i in range(5):
        rows = plane(i)
        for k in range(5):
            wide[i, k] = rows[:, k * 128 : (k + 1) * 128]
        for j in range(5):
            for k in range(5):
                put(at(i, j, k), wide[i, k, pl.ds(j, 8, stride=5), :])


def from_tiles(tile, put_plane, wide):
    for i in range(5):
        for j in range(5):
            for k in range(5):
                wide[i, k, pl.ds(j, 8, stride=5), :] = tile(i, j, k)
        for k in range(5):
            put_plane(i, k, wide[i, k])


def edge_slot(n):
    return n // 25 * 10 + (5 if n // 5 % 5 else 0) + n % 5


def patched(base, edge, *lead):
    def get(n):
        return edge[lead + (edge_slot(n),)] if n // 5 % 5 in (0, 4) else base[lead + (n,)]

    return get


def force(get, f, e, wm, source):
    def line(index, before):
        g = apply5(derivative, [get(n) for n in index])
        r = apply5(transposed, [g[a] * wm[index[a]] for a in range(5)])
        for a in range(5):
            f[e, index[a]] = before(index[a]) - r[a]

    for_lines(lambda index: line(index, source), directions[:1])
    for_lines(lambda index: line(index, lambda n: f[e, n]), directions[1:])


def fold(get, put, every=False):
    sub, ln = sublane(), lane()
    for i in range(5):
        v = [[get(at(i, j, k)) for k in range(5)] for j in range(5)]
        for k in range(5):
            v[0][k] = v[0][k] + jnp.where(sub == 0, 0.0, pltpu.roll(v[4][k], 1, 0))
        for j in range(5):
            v[j][0] = v[j][0] + jnp.where(ln == 0, 0.0, pltpu.roll(v[j][4], 1, 1))
        for j in range(5):
            for k in range(5):
                if every or j == 0 or k == 0:
                    put(at(i, j, k), v[j][k])


def emit_faces(get, c, face_low, face_high, row_low=None, row_high=None):
    lead = () if c is None else (c,)
    sub, ln = sublane(), lane()
    for i, face in ((0, face_low), (4, face_high)):
        last_row = jnp.zeros((8, 128), f32)
        last_column = jnp.zeros((8, 128), f32)
        for k in range(5):
            last_row = jnp.where(sub == k, row_of(get(at(i, 4, k)), 7), last_row)
        for j in range(4):
            last_column = jnp.where(ln == j, column_of(get(at(i, j, 4)), 127), last_column)
            for k in range(4):
                face[lead + (j * 4 + k,)] = get(at(i, j, k))
        face[lead + (16,)] = last_row
        face[lead + (17,)] = last_column
    for i in range(5) if row_low is not None else ():
        low = jnp.zeros((8, 128), f32)
        high = jnp.zeros((8, 128), f32)
        for k in range(5):
            low = jnp.where(sub == k, row_of(get(at(i, 0, k)), 0), low)
            high = jnp.where(sub == k, row_of(get(at(i, 4, k)), 7), high)
        row_low[lead + (i,)] = low
        row_high[lead + (i,)] = high


def complete(get, i, c, flags, from_below, from_above):
    sub, ln = sublane(), lane()
    v = [[get(at(i, j, k)) for k in range(5)] for j in range(5)]
    if i in (0, 4):
        face = from_below if i == 0 else from_above
        keep = flags[0 if i == 0 else 1] > 0
        for j in range(4):
            for k in range(4):
                v[j][k] = v[j][k] + jnp.where(keep, face[c, j * 4 + k], 0.0)
        last_row, last_column = face[c, 16], face[c, 17]
        for k in range(5):
            v[4][k] = v[4][k] + jnp.where((sub == 7) & keep, row_of(last_row, k), 0.0)
        for j in range(4):
            v[j][4] = v[j][4] + jnp.where((ln == 127) & keep, column_of(last_column, j), 0.0)
    for k in range(5):
        v[4][k] = jnp.where(sub == 7, v[4][k], pltpu.roll(v[0][k], 7, 0))
    for j in range(5):
        v[j][4] = jnp.where(ln == 127, v[j][4], pltpu.roll(v[j][0], 127, 1))
    return v


def sides(flags, from_even, from_odd, *index):
    even, odd = from_even[index], from_odd[index]
    return jnp.where(flags[4] > 0, odd, even), jnp.where(flags[4] > 0, even, odd)


def send_sides(flags, even_out, odd_out, index, low, high):
    even_out[index] = jnp.where(flags[4] > 0, high, low)
    odd_out[index] = jnp.where(flags[4] > 0, low, high)


def stack_rows(rows, first=0, tile=None):
    sub = sublane()
    tile = jnp.zeros((8, 128), f32) if tile is None else tile
    for n, (source, index) in enumerate(rows):
        tile = jnp.where(sub == first + n, row_of(source, index), tile)
    return tile


def pack_kernel(traces_in, owner_in, point_in, out, traces, owner, point, sems):
    pairs = ((traces_in, traces), (owner_in, owner), (point_in, point))
    copies = [pltpu.make_async_copy(a, b, sems.at[n]) for n, (a, b) in enumerate(pairs)]
    for copy in copies:
        copy.start()
    for copy in copies:
        copy.wait()
    devices = out.shape[0] // 2
    receivers = owner.shape[1]
    p = point[...]
    hi = p >> 7
    lo = p & 127

    def divide(x, by):
        return jnp.floor((x.astype(f32) + 0.5) * (1.0 / by)).astype(jnp.int32)

    t = divide(hi, 5)
    k = hi - 5 * t
    i = divide(t, 40)
    row = t - 40 * i
    ey = divide(row, 5)
    j = row - 5 * ey
    place = ((((i * 5 + j) * 5 + k) * 8 + ey) * 128 + lo).astype(f32)
    rows = [traces[0, 0:1, :], traces[0, 1:2, :], place, traces[1, 0:1, :]]
    rows += [traces[1, 1:2, :], traces[2, 0:1, :], traces[2, 1:2, :], jnp.zeros((1, receivers), f32)]
    owned = lax.broadcasted_iota(jnp.int32, (devices, receivers), 0) == owner[...]
    owned = jnp.where(owned, 1.0, 0.0)
    before = lax.broadcasted_iota(jnp.int32, (128, 128), 0) < lax.broadcasted_iota(jnp.int32, (128, 128), 1)
    before = jnp.where(before, 1.0, 0.0).astype(bf16)
    carry = jnp.zeros((devices, 1), f32)
    ranks = []
    for chunk in range(receivers // 128):
        part = owned[:, chunk * 128 : (chunk + 1) * 128]
        earlier = jnp.dot(part.astype(bf16), before, preferred_element_type=f32) + carry
        ranks.append(jnp.sum(part * earlier, axis=0, keepdims=True))
        carry = carry + jnp.sum(part, axis=1, keepdims=True)
    rank = jnp.concatenate(ranks, axis=1).astype(jnp.int32)
    chosen = lax.broadcasted_iota(jnp.int32, (slots, receivers), 0) == rank
    owned = owned.astype(bf16)
    total = jnp.zeros((devices, 256), f32)
    left = rows
    for _ in range(3):
        pieces = [v.astype(bf16) for v in left]
        left = [v - q.astype(f32) for v, q in zip(left, pieces)]
        table = jnp.concatenate([jnp.where(chosen, q.astype(f32), 0.0) for q in pieces], axis=0)
        total = total + lax.dot_general(
            owned, table.astype(bf16), (((1,), (1,)), ((), ())), preferred_element_type=f32
        )
    out[pl.ds(0, devices, stride=2), :] = total[:, :128]
    out[pl.ds(1, devices, stride=2), :] = total[:, 128:]


def scatter(places, values, hi_rows, lo_rows, piece_rows, left_side, right_side, store):
    place = places.astype(jnp.int32)
    hi_rows[...] = (place >> 7).astype(f32)
    lo_rows[...] = (place & 127).astype(f32)
    count = len(values)
    for c, v in enumerate(values):
        upper = v.astype(bf16).astype(f32)
        piece_rows[2 * c] = upper
        piece_rows[2 * c + 1] = v - upper
    index = [lax.broadcasted_iota(jnp.int32, (16, 128), 0).astype(f32) + 16.0 * g for g in range(8)]
    index = [x.astype(bf16) for x in index]
    one, zero = jnp.ones((16, 128), bf16), jnp.zeros((16, 128), bf16)

    def fill_right(r):
        where = slice(r * 128, r * 128 + 128)
        lo = jnp.broadcast_to(lo_rows[r : r + 1, :], (16, 128)).astype(bf16)
        pieces = [jnp.broadcast_to(piece_rows[n, r : r + 1, :], (16, 128)).astype(bf16) for n in range(2 * count)]
        for g in range(8):
            same = index[g] == lo
            for n in range(2 * count):
                at_row = n * 128 + g * 16
                right_side[at_row : at_row + 16, where] = jnp.where(same, pieces[n], zero)

    def fill_left(r, m):
        where = slice(r * 128, r * 128 + 128)
        hi = jnp.broadcast_to(hi_rows[r : r + 1, :], (16, 128))
        part = (hi - 128.0 * m).astype(bf16)
        for g in range(8):
            left_side[m * 128 + g * 16 : m * 128 + g * 16 + 16, where] = jnp.where(index[g] == part, one, zero)

    def fill_tile(m):
        for r in range(slots):
            fill_left(r, 2 * m)
            fill_left(r, 2 * m + 1)

    for r in range(slots):
        fill_right(r)
    fill_tile(0)
    for m in range(4):
        if m < 3:
            fill_tile(m + 1)
        for c in range(count):
            both = lax.dot_general(
                left_side[m * 256 : m * 256 + 256, :],
                right_side[c * 256 : c * 256 + 256, :],
                (((1,), (1,)), ((), ())),
                preferred_element_type=f32,
            )
            store(c, m, both[:, :128] + both[:, 128:])


def start_kernel(d_in, v_in, k_in, m_in, d_out, v_out, wm_out, mass_out, rim_out, kept, *scratch):
    d0, v0, modulus, density, d, v, wm, mass, rim, kd, edges, wide, sems = scratch
    copies = []

    def copy(source, target):
        copies.append(pltpu.make_async_copy(source, target, sems.at[len(copies)]))
        copies[-1].start()
        return copies[-1]

    loads = [copy(k_in, modulus), copy(d_in.at[0], d0.at[0]), copy(d_in.at[1], d0.at[1])]
    loads += [copy(m_in, density), copy(v_in, v0)]

    def weighted(target):
        def put(n, value):
            target[n] = value * weight(n // 25, n // 5 % 5, n % 5)

        return put

    loads[0].wait()
    to_tiles(lambda i: modulus[i].astype(f32), weighted(wm), wide)
    copy(wm, wm_out)
    for i in range(5):
        for j in range(5):
            tiles = [wm[at(i, j, k)] for k in range(5)]
            rim[0, i * 5 + j] = stack_rows([(tile, 0) for tile in tiles])
            rim[1, i * 5 + j] = stack_rows([(tile, 7) for tile in tiles])
    copy(rim, rim_out)
    for e in range(2):

        def put_d(n, value, e=e):
            d[e, n] = value

        loads[1 + e].wait()
        to_tiles(lambda i, e=e: d0[e, i], put_d, wide)
        copy(d.at[e], d_out.at[e])
        force(lambda n, e=e: d[e, n], kd, e, wm, lambda n: 0.0)
        copy(kd.at[e], kept.at[e * points : e * points + points])
    loads[3].wait()
    to_tiles(lambda i: density[i].astype(f32), weighted(mass), wide)

    def put_mass(n, value):
        mass[n] = value

    fold(lambda n: mass[n], put_mass)
    copy(mass, mass_out)
    low, high, row_low, row_high = edges.at[0:18], edges.at[18:36], edges.at[36:41], edges.at[41:46]
    emit_faces(lambda n: mass[n], None, low, high, row_low, row_high)
    copy(edges, kept.at[2 * points : 2 * points + 46])
    loads[4].wait()
    for e in range(2):

        def put_v(n, value, e=e):
            v[e, n] = value

        to_tiles(lambda i, e=e: v0[e, i], put_v, wide)
        copy(v.at[e], v_out.at[e])
    for pending in copies[len(loads) :]:
        pending.wait()


def first_force_kernel(got, kept, f, face_low, face_high, row_low, row_high, kd, sems, *scratch):
    edges = kept.at[2 * points : 2 * points + 46]
    pairs = ((kept.at[0:points], kd.at[0]), (kept.at[points : 2 * points], kd.at[1]))
    pairs += ((edges.at[0:18], face_low.at[2]), (edges.at[18:36], face_high.at[2]))
    pairs += ((edges.at[36:41], row_low.at[2]), (edges.at[41:46], row_high.at[2]))
    copies = [pltpu.make_async_copy(a, b, sems.at[n]) for n, (a, b) in enumerate(pairs)]
    for copy in copies:
        copy.start()
    devices = got.shape[0] // 2
    first = got[pl.ds(0, devices, stride=2), :].T

    def store(c, m, value):
        count = min(32, points - 32 * m)
        f[c, 32 * m : 32 * m + count] = value.reshape(32, 8, 128)[:count]

    scatter(first[64:96], [first[0:32], first[32:64]], *scratch, store)
    for copy in copies:
        copy.wait()

    def event(e, carry):
        def put(n, value):
            f[e, n] = value

        fold(lambda n: f[e, n] + kd[e, n], put, every=True)
        emit_faces(lambda n: f[e, n], e, face_low, face_high, row_low, row_high)
        return carry

    lax.fori_loop(0, 2, event, 0)


def source_kernel(step, got, order, s, token, *scratch):
    devices = got.shape[0] // 2
    first = got[pl.ds(0, devices, stride=2), :].T
    second = got[pl.ds(1, devices, stride=2), :].T
    token[...] = jnp.zeros_like(token)

    def store(c, m, value):
        s[c, 32 * m : 32 * m + 32] = value.reshape(32, 8, 128)

    values = [first[96:128], second[0:32]] if step == 1 else [second[32:64], second[64:96]]
    scatter(first[64:96], values, *scratch, store)


def rows_kernel(flags, from_below, from_above, row_low, row_high, wm_rim, order, even_out, odd_out, own):
    sub, ln = sublane(), lane()
    low_tiles = [wm_rim[0, n] for n in range(25)]
    high_tiles = [wm_rim[1, n] for n in range(25)]
    for c in range(row_low.shape[0]):
        for i in range(5):
            low, high = row_low[c, i], row_high[c, i]
            if i in (0, 4):
                face = from_below if i == 0 else from_above
                keep = flags[0 if i == 0 else 1] > 0
                extra = stack_rows([(face[c, k], 0) for k in range(4)])
                corner = jnp.broadcast_to(face[c, 17][0:1, 0:1], (8, 128))
                extra = jnp.where((sub == 4) & (ln == 127), corner, extra)
                low = low + jnp.where(keep, extra, 0.0)
                high = high + jnp.where(keep, face[c, 16], 0.0)
            shared = (sub == 4) & (ln < 127)
            low = jnp.where(shared, pltpu.roll(row_of(low, 0), 127, 1), low)
            high = jnp.where(shared, pltpu.roll(row_of(high, 0), 127, 1), high)
            own[0, c * 5 + i] = low
            own[1, c * 5 + i] = high
            for k in range(5):
                tile, where = packed_row(c, i, k)
                low_tiles[tile] = jnp.where(sub == where, row_of(low, k), low_tiles[tile])
                high_tiles[tile] = jnp.where(sub == where, row_of(high, k), high_tiles[tile])
    for n in range(25):
        send_sides(flags, even_out, odd_out, n, low_tiles[n], high_tiles[n])


def packed_row(c, i, k):
    row = (c * 5 + i) * 5 + k
    return row // 3, 5 + row % 3


def first_guess_kernel(flags, f, below, above, d, q, source, wm, mass, order, d_out, q_out, inverse, f_out):
    for i in range(5):
        v = complete(lambda n: mass[n], i, 2, flags, below, above)
        for j in range(5):
            for k in range(5):
                inverse[at(i, j, k)] = 1.0 / v[j][k]

    def event(e, carry):
        for i in range(5):
            v = complete(lambda n: f[e, n], i, e, flags, below, above)
            for j in range(5):
                for k in range(5):
                    n = at(i, j, k)
                    q_new = q[e, n] + 0.5 * time_step * (v[j][k] * inverse[n])
                    q_out[e, n] = q_new
                    d_out[e, n] = d[e, n] + time_step * q_new
        force(lambda n: d_out[e, n], f_out, e, wm, lambda n: source[e, n])
        return carry

    lax.fori_loop(0, 2, event, 0)


def add_row(tile, edge, rows, k):
    return tile + jnp.where(sublane() == edge, row_of(rows, k), 0.0)


def row_change_force(change, wm, row):
    out = [[None] * 5 for _ in range(5)]
    gx = apply5(derivative, change)
    rx = apply5(transposed, [gx[i] * wm[i][row] for i in range(5)])
    for i in range(5):
        out[i] = apply5(transposed, [float(derivative[b, row]) * change[i] * wm[i][b] for b in range(5)])
        gz = along_sublanes(derivative, change[i])
        out[i][row] = out[i][row] + rx[i] + along_sublanes(transposed, gz * wm[i][row])
    return out


def fold_with_rims(f, e, change, f_out, face_low, face_high):
    sub = sublane()

    def get(n):
        i, j, k = n // 25, n // 5 % 5, n % 5
        both = jnp.where(sub == 0, row_of(change[0, i * 5 + j], k), 0.0)
        return f[e, n] - jnp.where(sub == 7, row_of(change[1, i * 5 + j], k), both)

    def put(n, value):
        f_out[e, n] = value

    fold(get, put, every=True)
    emit_faces(lambda n: f_out[e, n], e, face_low, face_high)


def first_fix_kernel(flags, even, odd, own, wm_rim, d, q, inverse, f, *refs):
    d_edge, q_edge, inverse_edge, inverse_rim, f_out, face_low, face_high, change = refs
    sub = sublane()
    message = [sides(flags, even, odd, n) for n in range(25)]

    def received(side, c, i):
        tile = jnp.zeros((8, 128), f32)
        for k in range(5):
            n, where = packed_row(c, i, k)
            tile = jnp.where(sub == k, row_of(message[n][side], where), tile)
        return jnp.where(flags[2 + side] > 0, tile, 0.0)

    for side in range(2):
        for i in range(5):
            mass = jnp.where(sub < 5, own[side, 10 + i] + received(side, 2, i), 1.0)
            inverse_rim[side, i] = 1.0 / mass
            for k in range(5):
                n = at(i, 4 * side, k)
                inverse_edge[edge_slot(n)] = jnp.where(sub == 7 * side, row_of(inverse_rim[side, i], k), inverse[n])
    for e in range(2):
        for side in range(2):
            shift = []
            for i in range(5):
                mine = own[side, e * 5 + i]
                before = mine * (1.0 / jnp.where(sub < 5, own[side, 10 + i], 1.0))
                after = (mine + received(side, e, i)) * inverse_rim[side, i]
                q_change = 0.5 * time_step * (after - before)
                shift.append(time_step * q_change)
                for k in range(5):
                    n = at(i, 4 * side, k)
                    q_edge[e, edge_slot(n)] = add_row(q[e, n], 7 * side, q_change, k)
                    d_edge[e, edge_slot(n)] = add_row(d[e, n], 7 * side, shift[i], k)
            w = [[wm_rim[side, i * 5 + j] for j in range(5)] for i in range(5)]
            r = row_change_force(shift, w, 4 * side)
            for i in range(5):
                for j in range(5):
                    change[side, i * 5 + j] = r[i][j]
        fold_with_rims(f, e, change, f_out, face_low, face_high)


def advance_kernel(flags, f, below, above, d, d_edge, q, q_edge, inverse, inverse_edge, source, *refs):
    d_out, q_out, even_out, odd_out = refs
    get_inverse = patched(inverse, inverse_edge)

    def event(e, carry):
        get_d, get_q = patched(d, d_edge, e), patched(q, q_edge, e)
        for i in range(5):
            v = complete(lambda n: f[e, n], i, e, flags, below, above)
            new = [[None] * 5 for _ in range(5)]
            for j in range(5):
                for k in range(5):
                    n = at(i, j, k)
                    q_new = get_q(n) + time_step * (v[j][k] * get_inverse(n))
                    q_out[e, n] = q_new
                    new[j][k] = get_d(n) + time_step * q_new
                    d_out[e, n] = new[j][k]
            for m in range(4):
                low = stack_rows([(new[m + 1][k], 0) for k in range(5)])
                high = stack_rows([(new[m][k], 7) for k in range(5)])
                which = range(3) if m % 2 == 0 else range(3, 5)
                if m < 2:
                    low = stack_rows([(v[0][k], 0) for k in which], 5, low)
                    high = stack_rows([(v[4][k], 7) for k in which], 5, high)
                else:
                    low = stack_rows([(source[e, at(i, 0, k)], 0) for k in which], 5, low)
                    high = stack_rows([(source[e, at(i, 4, k)], 7) for k in which], 5, high)
                send_sides(flags, even_out, odd_out, (e, i * 4 + m), low, high)
        return carry

    lax.fori_loop(0, 2, event, 0)


def second_guess_kernel(d, source, wm, order, f_out):
    def event(e, carry):
        force(lambda n: d[e, n], f_out, e, wm, lambda n: source[e, n])
        return carry

    lax.fori_loop(0, 2, event, 0)


def along_sublanes(matrix, tile):
    sub = sublane()
    total = None
    for n in range(5):
        weights = jnp.zeros((8, 128), f32)
        for m in range(5):
            weights = jnp.where(sub == m, float(matrix[m, n]), weights)
        term = weights * row_of(tile, n)
        total = term if total is None else total + term
    return total


def rim_force(u, wm, near):
    out = []
    gx = apply5(derivative, [u[i][near] for i in range(5)])
    rx = apply5(transposed, [gx[i] * wm[i][near] for i in range(5)])
    for i in range(5):
        gy = apply5(derivative, u[i])
        ry = apply5(transposed, [gy[j] * wm[i][j] for j in range(5)])[near]
        gz = along_sublanes(derivative, u[i][near])
        rz = along_sublanes(transposed, gz * wm[i][near])
        out.append(rx[i] + ry + rz)
    return out


def second_fix_kernel(flags, even, odd, wm_even, wm_odd, wm_rim, inverse_rim, d, q, f, order, *refs):
    d_edge, q_edge, f_out, face_low, face_high, change = refs
    sub = sublane()
    wm_sides = [sides(flags, wm_even, wm_odd, n) for n in range(25)]
    for e in range(2):
        for side in range(2):
            keep = flags[2 + side] > 0
            shared, shift, u, w, sources = [], [], [], [], []
            for i in range(5):
                m = [sides(flags, even, odd, e, i * 4 + n)[side] for n in range(4)]
                forces = jnp.where(sub < 3, pltpu.roll(m[0], 3, 0), pltpu.roll(m[1], 6, 0))
                sources.append(jnp.where(sub < 3, pltpu.roll(m[2], 3, 0), pltpu.roll(m[3], 6, 0)))
                q_change = time_step * (jnp.where(keep & (sub < 5), forces, 0.0) * inverse_rim[side, i])
                shift.append(time_step * q_change)
                for k in range(5):
                    n = at(i, 4 * side, k)
                    q_edge[e, edge_slot(n)] = add_row(q[e, n], 7 * side, q_change, k)
                    d_edge[e, edge_slot(n)] = add_row(d[e, n], 7 * side, shift[i], k)
                here = stack_rows([(d_edge[e, edge_slot(at(i, 4 * side, k))], 7 * side) for k in range(5)])
                u.append([here] + m if side else m + [here])
                w.append([wm_sides[i * 5 + j][side] for j in range(5)])
            beyond = rim_force(u, w, 4 - 4 * side)
            w = [[wm_rim[side, i * 5 + j] for j in range(5)] for i in range(5)]
            r = row_change_force(shift, w, 4 * side)
            for i in range(5):
                r[i][4 * side] = r[i][4 * side] + jnp.where(keep, beyond[i] - sources[i], 0.0)
                for j in range(5):
                    change[side, i * 5 + j] = r[i][j]
        fold_with_rims(f, e, change, f_out, face_low, face_high)


def write_velocity(planes, flags, f, below, above, q, q_edge, inverse, inverse_edge, velocity, wide, rows, sems):
    get_inverse = patched(inverse, inverse_edge)
    copies = []
    for e in range(2):
        get_q = patched(q, q_edge, e)
        for m, i in enumerate(planes):
            v = complete(lambda n: f[e, n], i, e, flags, below, above)
            for j in range(5):
                for k in range(5):
                    n = at(i, j, k)
                    wide[i, k, pl.ds(j, 8, stride=5), :] = get_q(n) + 0.5 * time_step * (v[j][k] * get_inverse(n))
            for k in range(5):
                rows[e, m, :, k * 128 : (k + 1) * 128] = wide[i, k]
            copies.append(pltpu.make_async_copy(rows.at[e, m], velocity.at[e, i], sems.at[len(copies)]))
            copies[-1].start()
    for copy in copies:
        copy.wait()


def inner_velocity_kernel(f, q, q_edge, inverse, inverse_edge, order, velocity, token, *scratch):
    token[...] = jnp.zeros_like(token)
    write_velocity((1, 2, 3), None, f, None, None, q, q_edge, inverse, inverse_edge, velocity, *scratch)


def outer_velocity_kernel(flags, f, below, above, q, q_edge, inverse, inverse_edge, inner, order, velocity, *scratch):
    write_velocity((0, 4), flags, f, below, above, q, q_edge, inverse, inverse_edge, velocity, *scratch)


def correlate(d, d_edge, forward, step, total, wide, tiles):
    def event(e, carry):
        def put(n, value):
            tiles[n] = value

        to_tiles(lambda i: forward[step, e, i].astype(f32), put, wide)

        get_d = patched(d, d_edge, e)

        def line(index):
            g = apply5(derivative, [get_d(n) for n in index])
            h = apply5(derivative, [tiles[n] for n in index])
            for a in range(5):
                total[index[a]] = total[index[a]] + g[a] * h[a]

        for_lines(line, directions)
        return carry

    lax.fori_loop(0, 2, event, 0)


def first_term_kernel(d, d_edge, forward, order, total, token, wide, tiles):
    def clear(n, carry):
        total[n] = jnp.zeros((8, 128), f32)
        return carry

    lax.fori_loop(0, points, clear, 0)
    correlate(d, d_edge, forward, 0, total, wide, tiles)
    token[...] = jnp.zeros_like(token)


def last_term_kernel(d, d_edge, forward, before, wm, out, token, total, wide, tiles):
    def copy(n, carry):
        total[n] = before[n]
        return carry

    lax.fori_loop(0, points, copy, 0)
    correlate(d, d_edge, forward, 1, total, wide, tiles)
    token[...] = jnp.zeros_like(token)

    def tile(i, j, k):
        return total[at(i, j, k)] * wm[at(i, j, k)] * (-time_step / weight(i, j, k))

    def put_plane(i, k, rows):
        out[i, :, k * 128 : (k + 1) * 128] = rows

    from_tiles(tile, put_plane, wide)


def call(kernel, name, out_shapes, args, scratch=(), specs=None, outs=None, flops=10**6, moved=4 * 10**6, vmem=16, **more):
    return pl.pallas_call(
        kernel,
        name=name,
        out_shape=[s if hasattr(s, "dtype") else jax.ShapeDtypeStruct(s, f32) for s in out_shapes],
        in_specs=specs or [VMEM] * len(args),
        out_specs=outs or [VMEM] * len(out_shapes),
        scratch_shapes=list(scratch),
        compiler_params=pltpu.CompilerParams(vmem_limit_bytes=vmem * 2**20),
        cost_estimate=pl.CostEstimate(flops=flops, bytes_accessed=moved, transcendentals=0),
        **more,
    )(*args)


def swap(low, high, axis):
    count = lax.axis_size(axis)
    up = [(n, (n + 1) % count) for n in range(count)]
    down = [(b, a) for a, b in up]
    return lax.ppermute(high, axis, up), lax.ppermute(low, axis, down)


def on_device(d0, v0, modulus, density, forward, traces, owner, point):
    lat, lon = lax.axis_index("lat"), lax.axis_index("lon")
    lat_count, lon_count = lax.axis_size("lat"), lax.axis_size("lon")
    devices = lat_count * lon_count
    flags = [lat > 0, lat < lat_count - 1, lon > 0, lon < lon_count - 1, lon % 2 == 0]
    flags = jnp.stack(flags).astype(jnp.int32)
    field = (2, points, 8, 128)
    one = (points, 8, 128)
    wide_field = (2, padded, 8, 128)
    token = (8, 128)
    native = d0.shape
    d0, v0 = d0.reshape(2, 5, 40, 640), v0.reshape(2, 5, 40, 640)
    kernel_shape = modulus.shape
    modulus, density = modulus.reshape(5, 40, 640), density.reshape(5, 40, 640)
    forward = forward.reshape(2, 2, 5, 40, 640)
    receivers = owner.shape[0]

    def faces(channels):
        return [(channels, face_tiles, 8, 128)] * 2

    (packed,) = call(
        pack_kernel,
        "pack",
        [(2 * devices, 128)],
        (traces.transpose(1, 0, 2), owner.reshape(1, receivers), point.reshape(1, receivers)),
        [
            pltpu.VMEM((traces.shape[1], traces.shape[0], receivers), f32),
            pltpu.VMEM((1, receivers), jnp.int32),
            pltpu.VMEM((1, receivers), jnp.int32),
            pltpu.SemaphoreType.DMA((3,)),
        ],
        [HBM] * 3,
        vmem=56,
    )
    got = lax.all_to_all(packed.reshape(devices, 2, 128), ("lat", "lon"), 0, 0, tiled=True)
    got = got.reshape(2 * devices, 128)
    wide = pltpu.VMEM((5, 5, 40, 128), f32)
    tiles = pltpu.VMEM(one, f32)
    rim = (2, 25, 8, 128)
    d, q, wm, mass, wm_rim, kept = call(
        start_kernel,
        "start",
        [field, field, one, one, rim, (kept_tiles, 8, 128)],
        (d0, v0, modulus, density),
        [
            pltpu.VMEM(d0.shape, f32),
            pltpu.VMEM(v0.shape, f32),
            pltpu.VMEM(modulus.shape, bf16),
            pltpu.VMEM(density.shape, bf16),
        ]
        + [pltpu.VMEM(s, f32) for s in (field, field, one, one, rim, field, (46, 8, 128))]
        + [wide, pltpu.SemaphoreType.DMA((16,))],
        [HBM] * 4,
        [HBM] * 6,
        flops=10**8,
        vmem=56,
    )
    scatter_scratch = [
        pltpu.VMEM((slots, devices), f32),
        pltpu.VMEM((slots, devices), f32),
        pltpu.VMEM((4, slots, devices), f32),
        pltpu.VMEM((1024, slots * devices), bf16),
        pltpu.VMEM((512, slots * devices), bf16),
    ]
    f, *edges = call(
        first_force_kernel,
        "first_force",
        [field] + faces(3) + [(3, 5, 8, 128)] * 2,
        (got, kept),
        [pltpu.VMEM(field, f32), pltpu.SemaphoreType.DMA((6,))] + scatter_scratch,
        [VMEM, HBM],
        flops=4 * 10**9,
        vmem=18,
    )

    def source(step, order):
        return call(
            functools.partial(source_kernel, step),
            "source",
            [wide_field, token],
            (got, order),
            scatter_scratch,
            [VMEM, ANY],
            flops=4 * 10**9,
            vmem=18,
        )

    def trade(even, odd):
        pairs = [(n, n ^ 1) for n in range(lon_count)]
        between = [(n, (n + 1 if n % 2 else n - 1) % lon_count) for n in range(lon_count)]
        return lax.ppermute(even, "lon", pairs), lax.ppermute(odd, "lon", between)

    face_low, face_high, row_low, row_high = edges
    rim_fields = [(2, 50, 8, 128)] * 2
    s1, order = source(1, row_low)
    beside = swap(face_low, face_high, "lat")
    *message, own = call(
        rows_kernel,
        "rows",
        [(25, 8, 128)] * 2 + [(2, 15, 8, 128)],
        (flags, *beside, row_low, row_high, wm_rim, order),
        specs=[SMEM] + [VMEM] * 5 + [ANY],
        moved=4 * 10**5,
        vmem=4,
    )
    first_message = trade(*message)
    d1, q1, inverse, f = call(
        first_guess_kernel,
        "first_guess",
        [field, field, one, field],
        (flags, f, *beside, d, q, s1, wm, mass, message[0]),
        specs=[SMEM] + [VMEM] * 8 + [ANY],
        flops=10**8,
    )
    d1_edge, q1_edge, inverse_edge, inverse_rim, f, *edges = call(
        first_fix_kernel,
        "first_fix",
        rim_fields + [(50, 8, 128), (2, 5, 8, 128), field] + faces(2),
        (flags, *first_message, own, wm_rim, d1, q1, inverse, f),
        [pltpu.VMEM((2, 25, 8, 128), f32)],
        [SMEM] + [VMEM] * 8,
        flops=10**7,
    )
    s2, unused = source(2, edges[0])
    beside = swap(*edges, "lat")
    d2, q2, *message = call(
        advance_kernel,
        "advance",
        [field, field] + [(2, 20, 8, 128)] * 2,
        (flags, f, *beside, d1, d1_edge, q1, q1_edge, inverse, inverse_edge, s2),
        specs=[SMEM] + [VMEM] * 10,
        flops=10**7,
    )
    second_message = trade(*message)
    (f,) = call(
        second_guess_kernel,
        "second_guess",
        [field],
        (d2, s2, wm, message[0]),
        specs=[VMEM] * 3 + [ANY],
        flops=10**8,
    )
    term, order = call(
        first_term_kernel,
        "first_term",
        [one, token],
        (d1, d1_edge, forward, message[0]),
        [wide, tiles],
        [VMEM] * 3 + [ANY],
        flops=10**8,
    )
    d2_edge, q2_edge, f, *edges = call(
        second_fix_kernel,
        "second_fix",
        rim_fields + [field] + faces(2),
        (flags, *second_message, *first_message, wm_rim, inverse_rim, d2, q2, f, order),
        [pltpu.VMEM((2, 25, 8, 128), f32)],
        [SMEM] + [VMEM] * 9 + [ANY],
        flops=10**7,
    )
    beside = swap(*edges, "lat")
    kernel, order = call(
        last_term_kernel,
        "last_term",
        [(5, 40, 640), token],
        (d2, d2_edge, forward, term, wm),
        [tiles, wide, tiles],
        flops=10**8,
    )
    fields = (q2, q2_edge, inverse, inverse_edge)
    velocity, order_too = call(
        inner_velocity_kernel,
        "inner_velocity",
        [(2, 5, 40, 640), token],
        (f, *fields, order),
        [wide, pltpu.VMEM((2, 3, 40, 640), f32), pltpu.SemaphoreType.DMA((6,))],
        [VMEM] * 5 + [ANY],
        [HBM, VMEM],
        flops=10**7,
    )
    (velocity,) = call(
        outer_velocity_kernel,
        "outer_velocity",
        [(2, 5, 40, 640)],
        (flags, f, *beside, *fields, velocity, order_too),
        [wide, pltpu.VMEM((2, 2, 40, 640), f32), pltpu.SemaphoreType.DMA((4,))],
        [SMEM] + [VMEM] * 7 + [HBM, ANY],
        [HBM],
        flops=10**7,
        input_output_aliases={8: 0},
    )
    return velocity.reshape(native), kernel.reshape(kernel_shape)


def solution(mesh):
    placed = (
        P(None, "lat", None, "lon", None),
        P(None, "lat", None, "lon", None),
        P("lat", None, "lon", None),
        P("lat", None, "lon", None),
        P(None, None, "lat", None, "lon", None),
        P(None, None, ("lat", "lon")),
        P(("lat", "lon")),
        P(("lat", "lon")),
    )
    return jax.shard_map(
        on_device,
        mesh=mesh,
        in_specs=placed,
        out_specs=(P(None, "lat", None, "lon", None), P("lat", None, "lon", None)),
        check_vma=False,
    )
```

```python
import functools
import math

import jax
import jax.numpy as jnp
import numpy as np
from jax import lax
from jax.experimental import pallas as pl
from jax.experimental.pallas import tpu as pltpu
from jax.sharding import PartitionSpec as P

time_step = 0.05
f32 = jnp.float32
bf16 = jnp.bfloat16
points = 125
padded = 128
slots = 32
face_tiles = 18
kept_tiles = 12288
VMEM = pl.BlockSpec(memory_space=pltpu.VMEM)
HBM = pl.BlockSpec(memory_space=pltpu.HBM)
ANY = pl.BlockSpec(memory_space=pl.ANY)


def gll_tables():
    root_value = math.sqrt(3.0 / 7.0)
    gll_points = np.array([-1.0, -root_value, 0.0, root_value, 1.0])
    gll_weights = np.array([0.1, 49.0 / 90.0, 32.0 / 45.0, 49.0 / 90.0, 0.1])
    legendre = (35.0 * gll_points**4 - 30.0 * gll_points**2 + 3.0) / 8.0
    derivative = np.zeros((5, 5))
    for a in range(5):
        for b in range(5):
            if a != b:
                derivative[a, b] = legendre[a] / legendre[b] / (gll_points[a] - gll_points[b])
    derivative[0, 0] = -5.0
    derivative[4, 4] = 5.0
    return derivative, gll_weights


derivative, gll_weights = gll_tables()
transposed = derivative.T


def weight(i, j, k):
    return float(gll_weights[i] * gll_weights[j] * gll_weights[k])


def apply5(matrix, u):
    odd = (u[0] - u[4], u[1] - u[3])
    even = (u[0] + u[4], u[1] + u[3])
    out = [None] * 5
    for a in (0, 1):
        p = float(0.5 * (matrix[a, 0] - matrix[a, 4])) * odd[0]
        p = p + float(0.5 * (matrix[a, 1] - matrix[a, 3])) * odd[1]
        m = float(0.5 * (matrix[a, 0] + matrix[a, 4])) * even[0]
        m = m + float(0.5 * (matrix[a, 1] + matrix[a, 3])) * even[1]
        m = m + float(matrix[a, 2]) * u[2]
        out[a] = p + m
        out[4 - a] = p - m
    out[2] = float(matrix[2, 0]) * odd[0] + float(matrix[2, 1]) * odd[1]
    return out


directions = ((5, 1, 25), (25, 1, 5), (25, 5, 1))


def for_lines(body, directions):
    for outer, inner, step in directions:
        for t in range(5):
            for line in range(5):
                base = t * outer + line * inner
                body([base + step * n for n in range(5)])


def sublane():
    return lax.broadcasted_iota(jnp.int32, (8, 128), 0)


def lane():
    return lax.broadcasted_iota(jnp.int32, (8, 128), 1)


def row_of(tile, index):
    return jnp.broadcast_to(tile[index : index + 1, :], (8, 128))


def column_of(tile, index):
    return jnp.broadcast_to(tile[:, index : index + 1], (8, 128))


def at(i, j, k):
    return (i * 5 + j) * 5 + k


def to_tiles(plane, put, wide):
    for i in range(5):
        rows = plane(i)
        for k in range(5):
            wide[i, k] = rows[:, k * 128 : (k + 1) * 128]
        for j in range(5):
            for k in range(5):
                put(at(i, j, k), wide[i, k, pl.ds(j, 8, stride=5), :])


def from_tiles(tile, put_plane, wide):
    for i in range(5):
        for j in range(5):
            for k in range(5):
                wide[i, k, pl.ds(j, 8, stride=5), :] = tile(i, j, k)
        for k in range(5):
            put_plane(i, k, wide[i, k])


def edge_slot(n):
    return n // 25 * 10 + (5 if n // 5 % 5 else 0) + n % 5


def patched(base, edge, *lead):
    def get(n):
        return edge[lead + (edge_slot(n),)] if n // 5 % 5 in (0, 4) else base[lead + (n,)]

    return get


def force(get, f, e, wm, source):
    def line(index, before):
        g = apply5(derivative, [get(n) for n in index])
        r = apply5(transposed, [g[a] * wm[index[a]] for a in range(5)])
        for a in range(5):
            f[e, index[a]] = before(index[a]) - r[a]

    for_lines(lambda index: line(index, source), directions[:1])
    for_lines(lambda index: line(index, lambda n: f[e, n]), directions[1:])


def fold(get, put, every=False):
    sub, ln = sublane(), lane()
    for i in range(5):
        v = [[get(at(i, j, k)) for k in range(5)] for j in range(5)]
        for k in range(5):
            v[0][k] = v[0][k] + jnp.where(sub == 0, 0.0, pltpu.roll(v[4][k], 1, 0))
        for j in range(5):
            v[j][0] = v[j][0] + jnp.where(ln == 0, 0.0, pltpu.roll(v[j][4], 1, 1))
        for j in range(5):
            for k in range(5):
                if every or j == 0 or k == 0:
                    put(at(i, j, k), v[j][k])


def emit_faces(get, c, face_low, face_high, row_low=None, row_high=None):
    lead = () if c is None else (c,)
    sub, ln = sublane(), lane()
    for i, face in ((0, face_low), (4, face_high)):
        last_row = jnp.zeros((8, 128), f32)
        last_column = jnp.zeros((8, 128), f32)
        for k in range(5):
            last_row = jnp.where(sub == k, row_of(get(at(i, 4, k)), 7), last_row)
        for j in range(4):
            last_column = jnp.where(ln == j, column_of(get(at(i, j, 4)), 127), last_column)
            for k in range(4):
                face[lead + (j * 4 + k,)] = get(at(i, j, k))
        face[lead + (16,)] = last_row
        face[lead + (17,)] = last_column
    for i in range(5) if row_low is not None else ():
        low = jnp.zeros((8, 128), f32)
        high = jnp.zeros((8, 128), f32)
        for k in range(5):
            low = jnp.where(sub == k, row_of(get(at(i, 0, k)), 0), low)
            high = jnp.where(sub == k, row_of(get(at(i, 4, k)), 7), high)
        row_low[lead + (i,)] = low
        row_high[lead + (i,)] = high


def complete(get, i, c, flags, from_below, from_above):
    sub, ln = sublane(), lane()
    v = [[get(at(i, j, k)) for k in range(5)] for j in range(5)]
    if i in (0, 4):
        face = from_below if i == 0 else from_above
        keep = flags[0 if i == 0 else 1] > 0
        for j in range(4):
            for k in range(4):
                v[j][k] = v[j][k] + jnp.where(keep, face[c, j * 4 + k], 0.0)
        last_row, last_column = face[c, 16], face[c, 17]
        for k in range(5):
            v[4][k] = v[4][k] + jnp.where((sub == 7) & keep, row_of(last_row, k), 0.0)
        for j in range(4):
            v[j][4] = v[j][4] + jnp.where((ln == 127) & keep, column_of(last_column, j), 0.0)
    for k in range(5):
        v[4][k] = jnp.where(sub == 7, v[4][k], pltpu.roll(v[0][k], 7, 0))
    for j in range(5):
        v[j][4] = jnp.where(ln == 127, v[j][4], pltpu.roll(v[j][0], 127, 1))
    return v


def sides(flags, from_even, from_odd, *index):
    even, odd = from_even[index], from_odd[index]
    return jnp.where(flags[4] > 0, odd, even), jnp.where(flags[4] > 0, even, odd)


def send_sides(flags, even_out, odd_out, index, low, high):
    even_out[index] = jnp.where(flags[4] > 0, high, low)
    odd_out[index] = jnp.where(flags[4] > 0, low, high)


def stack_rows(rows, first=0, tile=None):
    sub = sublane()
    tile = jnp.zeros((8, 128), f32) if tile is None else tile
    for n, (source, index) in enumerate(rows):
        tile = jnp.where(sub == first + n, row_of(source, index), tile)
    return tile


def pack_kernel(traces_in, owner_in, point_in, out, traces, owner, point, sems):
    pairs = ((traces_in, traces), (owner_in, owner), (point_in, point))
    copies = [pltpu.make_async_copy(a, b, sems.at[n]) for n, (a, b) in enumerate(pairs)]
    for copy in copies:
        copy.start()
    for copy in copies:
        copy.wait()
    devices = out.shape[0] // 2
    receivers = owner.shape[1]
    p = point[...]
    hi = p >> 7
    lo = p & 127

    def divide(x, by):
        return jnp.floor((x.astype(f32) + 0.5) * (1.0 / by)).astype(jnp.int32)

    t = divide(hi, 5)
    k = hi - 5 * t
    i = divide(t, 40)
    row = t - 40 * i
    ey = divide(row, 5)
    j = row - 5 * ey
    place = ((((i * 5 + j) * 5 + k) * 8 + ey) * 128 + lo).astype(f32)
    rows = [traces[0, 0:1, :], traces[0, 1:2, :], place, traces[1, 0:1, :]]
    rows += [traces[1, 1:2, :], traces[2, 0:1, :], traces[2, 1:2, :], jnp.zeros((1, receivers), f32)]
    owned = lax.broadcasted_iota(jnp.int32, (devices, receivers), 0) == owner[...]
    owned = jnp.where(owned, 1.0, 0.0)
    before = lax.broadcasted_iota(jnp.int32, (128, 128), 0) < lax.broadcasted_iota(jnp.int32, (128, 128), 1)
    before = jnp.where(before, 1.0, 0.0).astype(bf16)
    carry = jnp.zeros((devices, 1), f32)
    ranks = []
    for chunk in range(receivers // 128):
        part = owned[:, chunk * 128 : (chunk + 1) * 128]
        earlier = jnp.dot(part.astype(bf16), before, preferred_element_type=f32) + carry
        ranks.append(jnp.sum(part * earlier, axis=0, keepdims=True))
        carry = carry + jnp.sum(part, axis=1, keepdims=True)
    rank = jnp.concatenate(ranks, axis=1).astype(jnp.int32)
    chosen = lax.broadcasted_iota(jnp.int32, (slots, receivers), 0) == rank
    owned = owned.astype(bf16)
    total = jnp.zeros((devices, 256), f32)
    left = rows
    for _ in range(3):
        pieces = [v.astype(bf16) for v in left]
        left = [v - q.astype(f32) for v, q in zip(left, pieces)]
        table = jnp.concatenate([jnp.where(chosen, q.astype(f32), 0.0) for q in pieces], axis=0)
        total = total + lax.dot_general(
            owned, table.astype(bf16), (((1,), (1,)), ((), ())), preferred_element_type=f32
        )
    out[pl.ds(0, devices, stride=2), :] = total[:, :128]
    out[pl.ds(1, devices, stride=2), :] = total[:, 128:]


def scatter(places, values, hi_rows, lo_rows, piece_rows, left_side, right_side, store):
    place = places.astype(jnp.int32)
    hi_rows[...] = (place >> 7).astype(f32)
    lo_rows[...] = (place & 127).astype(f32)
    count = len(values)
    for c, v in enumerate(values):
        upper = v.astype(bf16).astype(f32)
        piece_rows[2 * c] = upper
        piece_rows[2 * c + 1] = v - upper
    index = [lax.broadcasted_iota(jnp.int32, (16, 128), 0).astype(f32) + 16.0 * g for g in range(8)]
    index = [x.astype(bf16) for x in index]
    one, zero = jnp.ones((16, 128), bf16), jnp.zeros((16, 128), bf16)

    def fill_right(r):
        where = slice(r * 128, r * 128 + 128)
        lo = jnp.broadcast_to(lo_rows[r : r + 1, :], (16, 128)).astype(bf16)
        pieces = [jnp.broadcast_to(piece_rows[n, r : r + 1, :], (16, 128)).astype(bf16) for n in range(2 * count)]
        for g in range(8):
            same = index[g] == lo
            for n in range(2 * count):
                at_row = n * 128 + g * 16
                right_side[at_row : at_row + 16, where] = jnp.where(same, pieces[n], zero)

    def fill_left(r, m):
        where = slice(r * 128, r * 128 + 128)
        hi = jnp.broadcast_to(hi_rows[r : r + 1, :], (16, 128))
        part = (hi - 128.0 * m).astype(bf16)
        for g in range(8):
            left_side[m * 128 + g * 16 : m * 128 + g * 16 + 16, where] = jnp.where(index[g] == part, one, zero)

    def fill_tile(m):
        for r in range(slots):
            fill_left(r, 2 * m)
            fill_left(r, 2 * m + 1)

    for r in range(slots):
        fill_right(r)
    fill_tile(0)
    for m in range(4):
        if m < 3:
            fill_tile(m + 1)
        for c in range(count):
            both = lax.dot_general(
                left_side[m * 256 : m * 256 + 256, :],
                right_side[c * 256 : c * 256 + 256, :],
                (((1,), (1,)), ((), ())),
                preferred_element_type=f32,
            )
            store(c, m, both[:, :128] + both[:, 128:])


def start_kernel(d_in, k_in, m_in, d_out, wm_out, mass_out, rim_out, kept, low_out, high_out, rows_out, *scratch):
    d0, modulus, density, d, wm, mass, rim, kd, low, high, rows, wide, sems = scratch
    copies = []

    def copy(source, target):
        copies.append(pltpu.make_async_copy(source, target, sems.at[len(copies)]))
        copies[-1].start()
        return copies[-1]

    loads = [copy(k_in, modulus), copy(d_in.at[0], d0.at[0]), copy(d_in.at[1], d0.at[1])]
    loads += [copy(m_in, density)]

    def weighted(target):
        def put(n, value):
            target[n] = value * weight(n // 25, n // 5 % 5, n % 5)

        return put

    loads[0].wait()
    to_tiles(lambda i: modulus[i].astype(f32), weighted(wm), wide)
    copy(wm, wm_out)
    for i in range(5):
        for j in range(5):
            tiles = [wm[at(i, j, k)] for k in range(5)]
            rim[0, i * 5 + j] = stack_rows([(tile, 0) for tile in tiles])
            rim[1, i * 5 + j] = stack_rows([(tile, 7) for tile in tiles])
    copy(rim, rim_out)
    for e in range(2):

        def put_d(n, value, e=e):
            d[e, n] = value

        loads[1 + e].wait()
        to_tiles(lambda i, e=e: d0[e, i], put_d, wide)
        copy(d.at[e], d_out.at[e])
        force(lambda n, e=e: d[e, n], kd, e, wm, lambda n: 0.0)
        copy(kd.at[e], kept.at[e * points : e * points + points])
    loads[3].wait()
    to_tiles(lambda i: density[i].astype(f32), weighted(mass), wide)

    def put_mass(n, value):
        mass[n] = value

    fold(lambda n: mass[n], put_mass)
    copy(mass, mass_out)
    emit_faces(lambda n: mass[n], 0, low, high, rows.at[0:1], rows.at[1:2])
    copy(low, low_out)
    copy(high, high_out)
    copy(rows, rows_out)
    for pending in copies[len(loads) :]:
        pending.wait()


def first_force_kernel(got, kept, f, face_low, face_high, row_low, row_high, kd, sems, *scratch):
    copies = [pltpu.make_async_copy(kept.at[e * points : (e + 1) * points], kd.at[e], sems.at[e]) for e in range(2)]
    for copy in copies:
        copy.start()
    devices = got.shape[0] // 2
    first = got[pl.ds(0, devices, stride=2), :].T

    def store(c, m, value):
        count = min(32, points - 32 * m)
        f[c, 32 * m : 32 * m + count] = value.reshape(32, 8, 128)[:count]

    scatter(first[64:96], [first[0:32], first[32:64]], *scratch, store)
    for copy in copies:
        copy.wait()

    def event(e, carry):
        def put(n, value):
            f[e, n] = value

        fold(lambda n: f[e, n] + kd[e, n], put, every=True)
        emit_faces(lambda n: f[e, n], e, face_low, face_high, row_low, row_high)
        return carry

    lax.fori_loop(0, 2, event, 0)


def source_kernel(step, got, order, s, token, *scratch):
    devices = got.shape[0] // 2
    first = got[pl.ds(0, devices, stride=2), :].T
    second = got[pl.ds(1, devices, stride=2), :].T
    token[...] = jnp.zeros_like(token)

    def store(c, m, value):
        s[c, 32 * m : 32 * m + 32] = value.reshape(32, 8, 128)

    values = [first[96:128], second[0:32]] if step == 1 else [second[32:64], second[64:96]]
    scatter(first[64:96], values, *scratch, store)


def rows_kernel(flags, below, above, m_below, m_above, row_low, row_high, m_rows, wm_rim, order, *outs):
    even_out, odd_out, own = outs
    sub, ln = sublane(), lane()
    low_tiles = [wm_rim[0, n] for n in range(25)]
    high_tiles = [wm_rim[1, n] for n in range(25)]
    for c in range(3):
        for i in range(5):
            low, high = (row_low[c, i], row_high[c, i]) if c < 2 else (m_rows[0, i], m_rows[1, i])
            if i in (0, 4):
                face = (below if i == 0 else above) if c < 2 else (m_below if i == 0 else m_above)
                part = c if c < 2 else 0
                keep = flags[0 if i == 0 else 1] > 0
                extra = stack_rows([(face[part, k], 0) for k in range(4)])
                corner = jnp.broadcast_to(face[part, 17][0:1, 0:1], (8, 128))
                extra = jnp.where((sub == 4) & (ln == 127), corner, extra)
                low = low + jnp.where(keep, extra, 0.0)
                high = high + jnp.where(keep, face[part, 16], 0.0)
            shared = (sub == 4) & (ln < 127)
            low = jnp.where(shared, pltpu.roll(row_of(low, 0), 127, 1), low)
            high = jnp.where(shared, pltpu.roll(row_of(high, 0), 127, 1), high)
            own[0, c * 5 + i] = low
            own[1, c * 5 + i] = high
            for k in range(5):
                tile, where = packed_row(c, i, k)
                low_tiles[tile] = jnp.where(sub == where, row_of(low, k), low_tiles[tile])
                high_tiles[tile] = jnp.where(sub == where, row_of(high, k), high_tiles[tile])
    for n in range(25):
        send_sides(flags, even_out, odd_out, n, low_tiles[n], high_tiles[n])


def packed_row(c, i, k):
    row = (c * 5 + i) * 5 + k
    return row // 3, 5 + row % 3


def first_guess_kernel(flags, f, below, above, m_below, m_above, d, v0, source, wm, mass, order, *outs):
    d_out, q_out, inverse, f_out, wide = outs
    for i in range(5):
        v = complete(lambda n: mass[n], i, 0, flags, m_below, m_above)
        for j in range(5):
            for k in range(5):
                inverse[at(i, j, k)] = 1.0 / v[j][k]

    def event(e, carry):
        def put(n, value):
            q_out[e, n] = value

        to_tiles(lambda i: v0[e, i], put, wide)
        for i in range(5):
            v = complete(lambda n: f[e, n], i, e, flags, below, above)
            for j in range(5):
                for k in range(5):
                    n = at(i, j, k)
                    q_new = q_out[e, n] + 0.5 * time_step * (v[j][k] * inverse[n])
                    q_out[e, n] = q_new
                    d_out[e, n] = d[e, n] + time_step * q_new
        force(lambda n: d_out[e, n], f_out, e, wm, lambda n: source[e, n])
        return carry

    lax.fori_loop(0, 2, event, 0)


def add_row(tile, edge, rows, k):
    return tile + jnp.where(sublane() == edge, row_of(rows, k), 0.0)


def row_change_force(change, wm, row):
    out = [[None] * 5 for _ in range(5)]
    gx = apply5(derivative, change)
    rx = apply5(transposed, [gx[i] * wm[i][row] for i in range(5)])
    for i in range(5):
        out[i] = apply5(transposed, [float(derivative[b, row]) * change[i] * wm[i][b] for b in range(5)])
        gz = along_sublanes(derivative, change[i])
        out[i][row] = out[i][row] + rx[i] + along_sublanes(transposed, gz * wm[i][row])
    return out


def fold_with_rims(f, e, change, f_out, face_low, face_high):
    sub = sublane()

    def get(n):
        i, j, k = n // 25, n // 5 % 5, n % 5
        both = jnp.where(sub == 0, row_of(change[0, i * 5 + j], k), 0.0)
        return f[e, n] - jnp.where(sub == 7, row_of(change[1, i * 5 + j], k), both)

    def put(n, value):
        f_out[e, n] = value

    fold(get, put, every=True)
    emit_faces(lambda n: f_out[e, n], e, face_low, face_high)


def first_fix_kernel(flags, even, odd, own, wm_rim, d, q, inverse, f, *refs):
    d_edge, q_edge, inverse_edge, inverse_rim, f_out, face_low, face_high, change = refs
    sub = sublane()
    message = [sides(flags, even, odd, n) for n in range(25)]

    def received(side, c, i):
        tile = jnp.zeros((8, 128), f32)
        for k in range(5):
            n, where = packed_row(c, i, k)
            tile = jnp.where(sub == k, row_of(message[n][side], where), tile)
        return jnp.where(flags[2 + side] > 0, tile, 0.0)

    for side in range(2):
        for i in range(5):
            mass = jnp.where(sub < 5, own[side, 10 + i] + received(side, 2, i), 1.0)
            inverse_rim[side, i] = 1.0 / mass
            for k in range(5):
                n = at(i, 4 * side, k)
                inverse_edge[edge_slot(n)] = jnp.where(sub == 7 * side, row_of(inverse_rim[side, i], k), inverse[n])
    for e in range(2):
        for side in range(2):
            shift = []
            for i in range(5):
                mine = own[side, e * 5 + i]
                before = mine * (1.0 / jnp.where(sub < 5, own[side, 10 + i], 1.0))
                after = (mine + received(side, e, i)) * inverse_rim[side, i]
                q_change = 0.5 * time_step * (after - before)
                shift.append(time_step * q_change)
                for k in range(5):
                    n = at(i, 4 * side, k)
                    q_edge[e, edge_slot(n)] = add_row(q[e, n], 7 * side, q_change, k)
                    d_edge[e, edge_slot(n)] = add_row(d[e, n], 7 * side, shift[i], k)
            w = [[wm_rim[side, i * 5 + j] for j in range(5)] for i in range(5)]
            r = row_change_force(shift, w, 4 * side)
            for i in range(5):
                for j in range(5):
                    change[side, i * 5 + j] = r[i][j]
        fold_with_rims(f, e, change, f_out, face_low, face_high)


def advance_kernel(flags, f, below, above, d, d_edge, q, q_edge, inverse, inverse_edge, source, *refs):
    d_out, q_out, even_out, odd_out = refs
    get_inverse = patched(inverse, inverse_edge)

    def event(e, carry):
        get_d, get_q = patched(d, d_edge, e), patched(q, q_edge, e)
        for i in range(5):
            v = complete(lambda n: f[e, n], i, e, flags, below, above)
            new = [[None] * 5 for _ in range(5)]
            for j in range(5):
                for k in range(5):
                    n = at(i, j, k)
                    q_new = get_q(n) + time_step * (v[j][k] * get_inverse(n))
                    q_out[e, n] = q_new
                    new[j][k] = get_d(n) + time_step * q_new
                    d_out[e, n] = new[j][k]
            for m in range(4):
                low = stack_rows([(new[m + 1][k], 0) for k in range(5)])
                high = stack_rows([(new[m][k], 7) for k in range(5)])
                which = range(3) if m % 2 == 0 else range(3, 5)
                if m < 2:
                    low = stack_rows([(v[0][k], 0) for k in which], 5, low)
                    high = stack_rows([(v[4][k], 7) for k in which], 5, high)
                else:
                    low = stack_rows([(source[e, at(i, 0, k)], 0) for k in which], 5, low)
                    high = stack_rows([(source[e, at(i, 4, k)], 7) for k in which], 5, high)
                send_sides(flags, even_out, odd_out, (e, i * 4 + m), low, high)
        return carry

    lax.fori_loop(0, 2, event, 0)


def second_guess_kernel(d, source, wm, order, f_out):
    def event(e, carry):
        force(lambda n: d[e, n], f_out, e, wm, lambda n: source[e, n])
        return carry

    lax.fori_loop(0, 2, event, 0)


def along_sublanes(matrix, tile):
    sub = sublane()
    total = None
    for n in range(5):
        weights = jnp.zeros((8, 128), f32)
        for m in range(5):
            weights = jnp.where(sub == m, float(matrix[m, n]), weights)
        term = weights * row_of(tile, n)
        total = term if total is None else total + term
    return total


def rim_force(u, wm, near):
    out = []
    gx = apply5(derivative, [u[i][near] for i in range(5)])
    rx = apply5(transposed, [gx[i] * wm[i][near] for i in range(5)])
    for i in range(5):
        gy = apply5(derivative, u[i])
        ry = apply5(transposed, [gy[j] * wm[i][j] for j in range(5)])[near]
        gz = along_sublanes(derivative, u[i][near])
        rz = along_sublanes(transposed, gz * wm[i][near])
        out.append(rx[i] + ry + rz)
    return out


def second_fix_kernel(flags, even, odd, wm_even, wm_odd, wm_rim, inverse_rim, d, q, f, order, *refs):
    d_edge, q_edge, f_out, face_low, face_high, change = refs
    sub = sublane()
    wm_sides = [sides(flags, wm_even, wm_odd, n) for n in range(25)]
    for e in range(2):
        for side in range(2):
            keep = flags[2 + side] > 0
            shared, shift, u, w, sources = [], [], [], [], []
            for i in range(5):
                m = [sides(flags, even, odd, e, i * 4 + n)[side] for n in range(4)]
                forces = jnp.where(sub < 3, pltpu.roll(m[0], 3, 0), pltpu.roll(m[1], 6, 0))
                sources.append(jnp.where(sub < 3, pltpu.roll(m[2], 3, 0), pltpu.roll(m[3], 6, 0)))
                q_change = time_step * (jnp.where(keep & (sub < 5), forces, 0.0) * inverse_rim[side, i])
                shift.append(time_step * q_change)
                for k in range(5):
                    n = at(i, 4 * side, k)
                    q_edge[e, edge_slot(n)] = add_row(q[e, n], 7 * side, q_change, k)
                    d_edge[e, edge_slot(n)] = add_row(d[e, n], 7 * side, shift[i], k)
                here = stack_rows([(d_edge[e, edge_slot(at(i, 4 * side, k))], 7 * side) for k in range(5)])
                u.append([here] + m if side else m + [here])
                w.append([wm_sides[i * 5 + j][side] for j in range(5)])
            beyond = rim_force(u, w, 4 - 4 * side)
            w = [[wm_rim[side, i * 5 + j] for j in range(5)] for i in range(5)]
            r = row_change_force(shift, w, 4 * side)
            for i in range(5):
                r[i][4 * side] = r[i][4 * side] + jnp.where(keep, beyond[i] - sources[i], 0.0)
                for j in range(5):
                    change[side, i * 5 + j] = r[i][j]
        fold_with_rims(f, e, change, f_out, face_low, face_high)


def write_velocity(planes, flags, f, below, above, q, q_edge, inverse, inverse_edge, velocity, wide, rows, sems):
    get_inverse = patched(inverse, inverse_edge)
    copies = []
    for e in range(2):
        get_q = patched(q, q_edge, e)
        for m, i in enumerate(planes):
            v = complete(lambda n: f[e, n], i, e, flags, below, above)
            for j in range(5):
                for k in range(5):
                    n = at(i, j, k)
                    wide[i, k, pl.ds(j, 8, stride=5), :] = get_q(n) + 0.5 * time_step * (v[j][k] * get_inverse(n))
            for k in range(5):
                rows[e, m, :, k * 128 : (k + 1) * 128] = wide[i, k]
            copies.append(pltpu.make_async_copy(rows.at[e, m], velocity.at[e, i], sems.at[len(copies)]))
            copies[-1].start()
    for copy in copies:
        copy.wait()


def inner_velocity_kernel(f, q, q_edge, inverse, inverse_edge, order, velocity, token, *scratch):
    token[...] = jnp.zeros_like(token)
    write_velocity((1, 2, 3), None, f, None, None, q, q_edge, inverse, inverse_edge, velocity, *scratch)


def outer_velocity_kernel(flags, f, below, above, q, q_edge, inverse, inverse_edge, inner, order, velocity, *scratch):
    write_velocity((0, 4), flags, f, below, above, q, q_edge, inverse, inverse_edge, velocity, *scratch)


def correlate(d, d_edge, forward, step, total, wide, tiles):
    def event(e, carry):
        def put(n, value):
            tiles[n] = value

        to_tiles(lambda i: forward[step, e, i].astype(f32), put, wide)

        get_d = patched(d, d_edge, e)

        def line(index):
            g = apply5(derivative, [get_d(n) for n in index])
            h = apply5(derivative, [tiles[n] for n in index])
            for a in range(5):
                total[index[a]] = total[index[a]] + g[a] * h[a]

        for_lines(line, directions)
        return carry

    lax.fori_loop(0, 2, event, 0)


def first_term_kernel(d, d_edge, forward, order, total, token, wide, tiles):
    def clear(n, carry):
        total[n] = jnp.zeros((8, 128), f32)
        return carry

    lax.fori_loop(0, points, clear, 0)
    correlate(d, d_edge, forward, 0, total, wide, tiles)
    token[...] = jnp.zeros_like(token)


def last_term_kernel(d, d_edge, forward, before, wm, out, token, total, wide, tiles):
    def copy(n, carry):
        total[n] = before[n]
        return carry

    lax.fori_loop(0, points, copy, 0)
    correlate(d, d_edge, forward, 1, total, wide, tiles)
    token[...] = jnp.zeros_like(token)

    def tile(i, j, k):
        return total[at(i, j, k)] * wm[at(i, j, k)] * (-time_step / weight(i, j, k))

    def put_plane(i, k, rows):
        out[i, :, k * 128 : (k + 1) * 128] = rows

    from_tiles(tile, put_plane, wide)


def placed(kernel):
    def with_place(*refs):
        lat, lon = lax.axis_index("lat"), lax.axis_index("lon")
        lat_count, lon_count = lax.axis_size("lat"), lax.axis_size("lon")
        kernel((lat, lat_count - 1 - lat, lon, lon_count - 1 - lon, 1 - lon % 2), *refs)

    return with_place


def call(kernel, name, out_shapes, args, scratch=(), specs=None, outs=None, flops=10**6, moved=4 * 10**6, vmem=16, **more):
    return pl.pallas_call(
        kernel,
        name=name,
        out_shape=[s if hasattr(s, "dtype") else jax.ShapeDtypeStruct(s, f32) for s in out_shapes],
        in_specs=specs or [VMEM] * len(args),
        out_specs=outs or [VMEM] * len(out_shapes),
        scratch_shapes=list(scratch),
        compiler_params=pltpu.CompilerParams(vmem_limit_bytes=vmem * 2**20),
        cost_estimate=pl.CostEstimate(flops=flops, bytes_accessed=moved, transcendentals=0),
        **more,
    )(*args)


def swap(low, high, axis):
    count = lax.axis_size(axis)
    up = [(n, (n + 1) % count) for n in range(count)]
    down = [(b, a) for a, b in up]
    return lax.ppermute(high, axis, up), lax.ppermute(low, axis, down)


def on_device(d0, v0, modulus, density, forward, traces, owner, point):
    lat_count, lon_count = lax.axis_size("lat"), lax.axis_size("lon")
    devices = lat_count * lon_count
    field = (2, points, 8, 128)
    one = (points, 8, 128)
    wide_field = (2, padded, 8, 128)
    token = (8, 128)
    native = d0.shape
    d0, v0 = d0.reshape(2, 5, 40, 640), v0.reshape(2, 5, 40, 640)
    kernel_shape = modulus.shape
    modulus, density = modulus.reshape(5, 40, 640), density.reshape(5, 40, 640)
    forward = forward.reshape(2, 2, 5, 40, 640)
    receivers = owner.shape[0]

    def faces(channels):
        return [(channels, face_tiles, 8, 128)] * 2

    (packed,) = call(
        pack_kernel,
        "pack",
        [(2 * devices, 128)],
        (traces.transpose(1, 0, 2), owner.reshape(1, receivers), point.reshape(1, receivers)),
        [
            pltpu.VMEM((traces.shape[1], traces.shape[0], receivers), f32),
            pltpu.VMEM((1, receivers), jnp.int32),
            pltpu.VMEM((1, receivers), jnp.int32),
            pltpu.SemaphoreType.DMA((3,)),
        ],
        [HBM] * 3,
        vmem=56,
    )
    got = lax.all_to_all(packed.reshape(devices, 2, 128), ("lat", "lon"), 0, 0, tiled=True)
    got = got.reshape(2 * devices, 128)
    wide = pltpu.VMEM((5, 5, 40, 128), f32)
    tiles = pltpu.VMEM(one, f32)
    rim = (2, 25, 8, 128)
    d, wm, mass, wm_rim, kept, *mass_edges = call(
        start_kernel,
        "start",
        [field, one, one, rim, (kept_tiles, 8, 128)] + faces(1) + [(2, 5, 8, 128)],
        (d0, modulus, density),
        [
            pltpu.VMEM(d0.shape, f32),
            pltpu.VMEM(modulus.shape, bf16),
            pltpu.VMEM(density.shape, bf16),
        ]
        + [pltpu.VMEM(s, f32) for s in [field, one, one, rim, field] + faces(1) + [(2, 5, 8, 128)]]
        + [wide, pltpu.SemaphoreType.DMA((16,))],
        [HBM] * 3,
        [HBM] * 8,
        flops=10**8,
        vmem=56,
    )
    mass_beside = swap(*mass_edges[:2], "lat")
    scatter_scratch = [
        pltpu.VMEM((slots, devices), f32),
        pltpu.VMEM((slots, devices), f32),
        pltpu.VMEM((4, slots, devices), f32),
        pltpu.VMEM((1024, slots * devices), bf16),
        pltpu.VMEM((512, slots * devices), bf16),
    ]
    f, *edges = call(
        first_force_kernel,
        "first_force",
        [field] + faces(2) + [(2, 5, 8, 128)] * 2,
        (got, kept),
        [pltpu.VMEM(field, f32), pltpu.SemaphoreType.DMA((2,))] + scatter_scratch,
        [VMEM, HBM],
        flops=4 * 10**9,
        vmem=18,
    )

    def source(step, order):
        return call(
            functools.partial(source_kernel, step),
            "source",
            [wide_field, token],
            (got, order),
            scatter_scratch,
            [VMEM, ANY],
            flops=4 * 10**9,
            vmem=18,
        )

    def trade(even, odd):
        pairs = [(n, n ^ 1) for n in range(lon_count)]
        between = [(n, (n + 1 if n % 2 else n - 1) % lon_count) for n in range(lon_count)]
        return lax.ppermute(even, "lon", pairs), lax.ppermute(odd, "lon", between)

    face_low, face_high, row_low, row_high = edges
    rim_fields = [(2, 50, 8, 128)] * 2
    s1, order = source(1, row_low)
    beside = swap(face_low, face_high, "lat")
    *message, own = call(
        placed(rows_kernel),
        "rows",
        [(25, 8, 128)] * 2 + [(2, 15, 8, 128)],
        (*beside, *mass_beside, row_low, row_high, mass_edges[2], wm_rim, order),
        specs=[VMEM] * 8 + [ANY],
        moved=4 * 10**5,
        vmem=4,
    )
    first_message = trade(*message)
    d1, q1, inverse, f = call(
        placed(first_guess_kernel),
        "first_guess",
        [field, field, one, field],
        (f, *beside, *mass_beside, d, v0, s1, wm, mass, message[0]),
        [wide],
        [VMEM] * 10 + [ANY],
        flops=10**8,
    )
    d1_edge, q1_edge, inverse_edge, inverse_rim, f, *edges = call(
        placed(first_fix_kernel),
        "first_fix",
        rim_fields + [(50, 8, 128), (2, 5, 8, 128), field] + faces(2),
        (*first_message, own, wm_rim, d1, q1, inverse, f),
        [pltpu.VMEM((2, 25, 8, 128), f32)],
        [VMEM] * 8,
        flops=10**7,
    )
    s2, unused = source(2, edges[0])
    beside = swap(*edges, "lat")
    d2, q2, *message = call(
        placed(advance_kernel),
        "advance",
        [field, field] + [(2, 20, 8, 128)] * 2,
        (f, *beside, d1, d1_edge, q1, q1_edge, inverse, inverse_edge, s2),
        specs=[VMEM] * 10,
        flops=10**7,
    )
    second_message = trade(*message)
    (f,) = call(
        second_guess_kernel,
        "second_guess",
        [field],
        (d2, s2, wm, message[0]),
        specs=[VMEM] * 3 + [ANY],
        flops=10**8,
    )
    term, order = call(
        first_term_kernel,
        "first_term",
        [one, token],
        (d1, d1_edge, forward, message[0]),
        [wide, tiles],
        [VMEM] * 3 + [ANY],
        flops=10**8,
    )
    d2_edge, q2_edge, f, *edges = call(
        placed(second_fix_kernel),
        "second_fix",
        rim_fields + [field] + faces(2),
        (*second_message, *first_message, wm_rim, inverse_rim, d2, q2, f, order),
        [pltpu.VMEM((2, 25, 8, 128), f32)],
        [VMEM] * 9 + [ANY],
        flops=10**7,
    )
    beside = swap(*edges, "lat")
    kernel, order = call(
        last_term_kernel,
        "last_term",
        [(5, 40, 640), token],
        (d2, d2_edge, forward, term, wm),
        [tiles, wide, tiles],
        flops=10**8,
    )
    fields = (q2, q2_edge, inverse, inverse_edge)
    velocity, order_too = call(
        inner_velocity_kernel,
        "inner_velocity",
        [(2, 5, 40, 640), token],
        (f, *fields, order),
        [wide, pltpu.VMEM((2, 3, 40, 640), f32), pltpu.SemaphoreType.DMA((6,))],
        [VMEM] * 5 + [ANY],
        [HBM, VMEM],
        flops=10**7,
    )
    (velocity,) = call(
        placed(outer_velocity_kernel),
        "outer_velocity",
        [(2, 5, 40, 640)],
        (f, *beside, *fields, velocity, order_too),
        [wide, pltpu.VMEM((2, 2, 40, 640), f32), pltpu.SemaphoreType.DMA((4,))],
        [VMEM] * 7 + [HBM, ANY],
        [HBM],
        flops=10**7,
        input_output_aliases={7: 0},
    )
    return velocity.reshape(native), kernel.reshape(kernel_shape)


def solution(mesh):
    placed = (
        P(None, "lat", None, "lon", None),
        P(None, "lat", None, "lon", None),
        P("lat", None, "lon", None),
        P("lat", None, "lon", None),
        P(None, None, "lat", None, "lon", None),
        P(None, None, ("lat", "lon")),
        P(("lat", "lon")),
        P(("lat", "lon")),
    )
    return jax.shard_map(
        on_device,
        mesh=mesh,
        in_specs=placed,
        out_specs=(P(None, "lat", None, "lon", None), P("lat", None, "lon", None)),
        check_vma=False,
    )
```
